32 devices in a mesh: groups: 2 (over x), horiz: 4 (over y, core), level: 4 (over z).
Axes of the slice: x: 2, y: 2, z: 4, core: 2. Of those that a mesh axis runs over, the one named last changes fastest.
Arguments:
- fields: bfloat16 [8, 80, 32768], P(None, 'level', ('groups', 'horiz')), parts along dimension 2, may hold values from -6 to 6
- enc_in: bfloat16 [1024, 640], replicated, may hold values from -0.25 to 0.25
- enc_out: bfloat16 [1024, 64], replicated, may hold values from -0.1875 to 0.1875
- dec_in: bfloat16 [64, 1024], replicated, may hold values from -0.75 to 0.75
- dec_out: bfloat16 [1024, 640], replicated, may hold values from -0.1875 to 0.1875
- hyper_weight: bfloat16 [64, 128], replicated, may hold values from -1.5 to 1.5
- neighbours: int32 [6, 16384], P(None, ('horiz', 'level')), may hold values from 0 to 4352, as said below
- edge_rows: int32 [4, 2, 128], P('horiz'), may hold values from 0 to 4095, as said below
Outputs:
- grad_enc_in: float32 [2048, 640], P(('groups', 'horiz', 'level')), parts along dimension 0
- grad_enc_out: float32 [2048, 64], P('groups'), parts along dimension 0
- grad_dec_in: float32 [128, 1024], P('groups'), parts along dimension 0
- grad_dec_out: float32 [2048, 640], P(('groups', 'horiz', 'level')), parts along dimension 0
- grad_hyper: float32 [128, 128], P('groups'), parts along dimension 0
- cell_rate: float32 [32768], P(('groups', 'horiz', 'level')), parts along dimension 0
- loss: float32 [2], P('groups'), parts along dimension 0
The draws below stay inside these ranges and needn't reach their ends.
There are 2 independent parts, one for each index of `groups`. The reference program is written for one: setup_inputs(seed, part) draws one part's arguments, and reference() takes and returns one part's arrays. A program takes and returns all parts, laid end to end along the dimension named above; an argument that names none is the same for every part. Nothing has to cross between parts.
Inputs may be any that keep to these rules, and one draw needn't show every extreme that they name: `neighbours`: entries of cell c of partition p: below 4096 a position in partition p; 4096 + e reads slot e of the list edge_rows[p - 1, 1] of the previous partition; 4224 + e slot e of edge_rows[p + 1, 0] of the next partition (modulo 4); 4352 marks no neighbour. Every cell has 5 or 6 valid entries. The slots read of one list are its first ones, their number differs between lists, and some list is read in all 128 slots. `edge_rows`: positions within the partition; the entries of one partition's two lists are all distinct.
All inputs are finite; a program needn't handle non-finite values.
Results may differ from the reference program's by a relative error of at most 0.0038.
Values may be sent and summed in bfloat16 or wider, within the bound.
No kernel may reach another device: no remote copies, remote signals or barrier semaphores. Data moves between devices by JAX's collectives and lax.ppermute only.
A program may use at most 128 MiB of HBM per device.

```python
import math
import jax
import jax.numpy as jnp
from jax import lax

VARS = 8
LEVELS = 80
HIDDEN_SIZE = 1024
LATENT = 64
EDGE = 128
FEAT = 640
PART_CELLS = 4096
CELLS = 16384
N_HORIZ = 4


def place_ends(order):
    shifted = (order + (PART_CELLS - 1 - order[0])) % PART_CELLS
    position = jnp.argmax(shifted == 0)
    moved = shifted.at[position].set(shifted[EDGE - 1])
    return moved.at[EDGE - 1].set(0).astype(jnp.int32)


def shared_layout(key):
    parts = N_HORIZ
    order_keys = jax.random.split(jax.random.fold_in(key, 101), parts)
    orders = jax.vmap(lambda member_key: place_ends(jax.random.permutation(member_key, PART_CELLS).astype(jnp.int32)))(order_keys).astype(jnp.int32)
    lengths = jax.random.randint(jax.random.fold_in(key, 102), (parts,), EDGE // 2, EDGE + 1)
    fullest = jax.random.randint(jax.random.fold_in(key, 103), (), 0, parts)
    lengths = jnp.where(jnp.arange(parts) == fullest, EDGE, lengths).astype(jnp.int32)
    return (orders, lengths)


def draw_edge_rows(key, part):
    orders, lengths = shared_layout(key)
    strip = 2 * EDGE
    top_start = (PART_CELLS // strip - 1) * strip
    lower = orders[:, :EDGE]
    upper = orders[:, top_start:top_start + EDGE]
    return jnp.stack([lower, upper], axis=1).astype(jnp.int32)


def draw_neighbours(key, part):
    orders, lengths = shared_layout(key)
    key = jax.random.fold_in(key, 11)
    parts = N_HORIZ
    strip = 2 * EDGE
    rows_total = PART_CELLS // strip
    spatial = jnp.arange(PART_CELLS, dtype=jnp.int32)
    row_index = spatial // strip
    col_index = spatial % strip
    pentagons = jax.random.randint(key, (parts,), 0, PART_CELLS)
    above_lengths = jnp.roll(lengths, -1)

    def one_partition(order, low_length, high_length, pentagon):
        entries = []
        for row_step, col_step in ((0, -1), (0, 1), (-1, 0), (-1, 1), (1, 0), (1, -1)):
            target_row = row_index + row_step
            target_col = (col_index + col_step) % strip
            inside = (target_row >= 0) & (target_row < rows_total)
            clipped = jnp.clip(target_row, 0, rows_total - 1)
            own_cell = order[clipped * strip + target_col]
            from_below = PART_CELLS + target_col * low_length // strip
            from_above = PART_CELLS + EDGE + target_col * high_length // strip
            entries.append(jnp.where(inside, own_cell, jnp.where(target_row < 0, from_below, from_above)))
        entries[5] = jnp.where(spatial == pentagon, PART_CELLS + 2 * EDGE, entries[5])
        stacked = jnp.stack(entries, axis=0).astype(jnp.int32)
        return jnp.zeros((6, PART_CELLS), jnp.int32).at[:, order].set(stacked)
    per_partition = jax.vmap(one_partition)(orders, lengths, above_lengths, pentagons)
    return jnp.transpose(per_partition, (1, 0, 2)).reshape(6, parts * PART_CELLS).astype(jnp.int32)


def shard_levels(own_key, shape, shards, low, largest):
    level, own = 1.0, jax.random.fold_in(own_key, 6)
    for dim, blocks in shards:
        heights = jnp.exp(jax.random.uniform(jax.random.fold_in(own, dim), (blocks,), jnp.float32, low / len(shards), largest / len(shards)))
        level = level * jnp.repeat(heights, shape[dim] // blocks).reshape([-1 if axis == dim else 1 for axis in range(len(shape))])
    return level


def noise(key, shape, deviation, most, cuts=(), kind=jnp.bfloat16):
    array = deviation * jax.random.normal(key, shape, jnp.float32)
    if cuts:
        array = array * shard_levels(key, shape, cuts, -0.22, 0.18)
    return jnp.clip(array, -most, most).astype(kind)


def setup_inputs(seed: int = 0, part: int = 0) -> dict:
    keys = jax.random.split(jax.random.key(seed), 9)
    own_keys = jax.random.split(jax.random.fold_in(keys[8], part), 9)
    fields = noise(own_keys[0], (VARS, LEVELS, CELLS), 1.0, 6.0, ((1, 4), (2, 4)))
    enc_in = noise(keys[1], (HIDDEN_SIZE, FEAT), FEAT ** -0.5, 0.25)
    enc_out = noise(keys[2], (HIDDEN_SIZE, LATENT), HIDDEN_SIZE ** -0.5, 0.1875)
    dec_in = noise(keys[3], (LATENT, HIDDEN_SIZE), LATENT ** -0.5, 0.75)
    dec_out = noise(keys[4], (HIDDEN_SIZE, FEAT), HIDDEN_SIZE ** -0.5, 0.1875)
    hyper_weight = noise(keys[5], (LATENT, 2 * LATENT), 0.25, 1.5)
    neighbours = draw_neighbours(jax.random.fold_in(keys[8], 71), part)
    edge_rows = draw_edge_rows(jax.random.fold_in(keys[8], 71), part)
    return {"fields": fields, "enc_in": enc_in, "enc_out": enc_out, "dec_in": dec_in, "dec_out": dec_out, "hyper_weight": hyper_weight, "neighbours": neighbours, "edge_rows": edge_rows}


scale_offset = 0.1

def product(left, right, dims):
    return lax.dot_general(left.astype(jnp.float32), right.astype(jnp.float32), dims, preferred_element_type=jnp.float32)

def silu_slope(preact):
    squash = jax.nn.sigmoid(preact)
    return squash * (1.0 + preact * (1.0 - squash))

def context_mean(table, adjacency):
    limit = table.shape[1]
    valid = adjacency < limit
    safe = jnp.where(valid, adjacency, 0)
    total = jnp.zeros((table.shape[0], adjacency.shape[1]), jnp.float32)
    for neighbour in range(6):
        total = total + jnp.where(valid[neighbour][None, :], table[:, safe[neighbour]].astype(jnp.float32), 0.0)
    count = lax.optimization_barrier(jnp.sum(valid.astype(jnp.float32), axis=0))
    return (total / count, valid, safe, count)

def hyper_terms(latent, context, hyper_weight, grad_scale):
    context_b = context.astype(jnp.bfloat16)
    params = product(hyper_weight, context_b, (((0,), (0,)), ((), ())))
    width = latent.shape[0]
    centre = params[:width]
    spread = params[width:]
    sigma = scale_offset + jax.nn.softplus(spread)
    scaled = (latent.astype(jnp.float32) - centre) / sigma
    rate = lax.optimization_barrier(jnp.sum(0.5 * scaled * scaled + jnp.log(sigma), axis=0))
    direct = grad_scale * scaled / sigma
    d_spread = grad_scale * (1.0 - scaled * scaled) / sigma * jax.nn.sigmoid(spread)
    d_params = jnp.concatenate([-direct, d_spread], axis=0).astype(jnp.bfloat16)
    d_context = product(hyper_weight, d_params, (((1,), (0,)), ((), ())))
    return (rate, direct, context_b, d_params, d_context)

def spread_back(d_context, count, valid, safe, limit):
    share = d_context / count
    grad_table = jnp.zeros((share.shape[0], limit), jnp.float32)
    for neighbour in range(6):
        grad_table = grad_table.at[:, safe[neighbour]].add(jnp.where(valid[neighbour][None, :], share, 0.0))
    return grad_table

def reference(fields, enc_in, enc_out, dec_in, dec_out, hyper_weight, neighbours, edge_rows):
    columns_all = fields.reshape(FEAT, CELLS)
    grad_scale = 1.0 / math.sqrt(CELLS)
    contract_rows = (((0,), (0,)), ((), ()))
    contract_cells = (((1,), (1,)), ((), ()))
    plain = (((1,), (0,)), ((), ()))

    def first_pass(index):
        columns = lax.dynamic_slice_in_dim(columns_all, index * PART_CELLS, PART_CELLS, 1)
        pre_enc = product(enc_in, columns, plain)
        hidden_enc = jax.nn.silu(pre_enc).astype(jnp.bfloat16)
        latent = product(enc_out, hidden_enc, contract_rows).astype(jnp.bfloat16)
        pre_dec = product(dec_in, latent, contract_rows)
        hidden_dec = jax.nn.silu(pre_dec).astype(jnp.bfloat16)
        recon = product(dec_out, hidden_dec, contract_rows)
        residual = recon - columns.astype(jnp.float32)
        distortion = lax.optimization_barrier(jnp.sum(residual * residual, axis=0))
        d_recon = (2.0 * grad_scale * residual).astype(jnp.bfloat16)
        d_dec_out = product(hidden_dec, d_recon, contract_cells)
        d_hidden_dec = product(dec_out, d_recon, plain)
        d_pre_dec = (d_hidden_dec * silu_slope(pre_dec)).astype(jnp.bfloat16)
        d_dec_in = product(latent, d_pre_dec, contract_cells)
        d_latent = product(dec_in, d_pre_dec, plain)
        return (latent, d_latent, distortion, d_dec_out, d_dec_in)
    latents, d_latents, distortions, dec_out_terms, dec_in_terms = lax.map(first_pass, jnp.arange(N_HORIZ))
    to_lower = jax.vmap(lambda latent, rows: latent[:, rows])(latents, edge_rows[:, 0])
    to_upper = jax.vmap(lambda latent, rows: latent[:, rows])(latents, edge_rows[:, 1])
    tables = jnp.concatenate([latents, jnp.roll(to_upper, 1, 0), jnp.roll(to_lower, -1, 0)], axis=2)
    adjacency_parts = jnp.transpose(neighbours.reshape(6, N_HORIZ, PART_CELLS), (1, 0, 2))

    def second_pass(inputs):
        table, adjacency, latent = inputs
        context, valid, safe, count = context_mean(table, adjacency)
        rate, direct, context_b, d_params, d_context = hyper_terms(latent, context, hyper_weight, grad_scale)
        grad_table = spread_back(d_context, count, valid, safe, table.shape[1])
        d_hyper = product(context_b, d_params, contract_cells)
        return (rate, direct, grad_table, d_hyper)
    rates, directs, grad_tables, hyper_terms_all = lax.map(second_pass, (tables, adjacency_parts, latents))
    own = grad_tables[:, :, :PART_CELLS]
    from_next = jnp.roll(grad_tables[:, :, PART_CELLS + EDGE:], 1, 0)
    from_prev = jnp.roll(grad_tables[:, :, PART_CELLS:PART_CELLS + EDGE], -1, 0)
    own = jax.vmap(lambda block, rows, grads: block.at[:, rows].add(grads))(own, edge_rows[:, 0], from_next)
    own = jax.vmap(lambda block, rows, grads: block.at[:, rows].add(grads))(own, edge_rows[:, 1], from_prev)
    d_latent_total = (d_latents + directs + own).astype(jnp.bfloat16)

    def third_pass(index):
        columns = lax.dynamic_slice_in_dim(columns_all, index * PART_CELLS, PART_CELLS, 1)
        d_latent = d_latent_total[index]
        pre_enc = product(enc_in, columns, plain)
        hidden_enc = jax.nn.silu(pre_enc).astype(jnp.bfloat16)
        d_enc_out = product(hidden_enc, d_latent, contract_cells)
        d_hidden_enc = product(enc_out, d_latent, plain)
        d_pre_enc = (d_hidden_enc * silu_slope(pre_enc)).astype(jnp.bfloat16)
        d_enc_in = product(d_pre_enc, columns, contract_cells)
        return (d_enc_in, d_enc_out)
    enc_in_terms, enc_out_terms = lax.map(third_pass, jnp.arange(N_HORIZ))
    grad_enc_in = lax.optimization_barrier(jnp.sum(enc_in_terms, axis=0))
    grad_enc_out = lax.optimization_barrier(jnp.sum(enc_out_terms, axis=0))
    grad_dec_in = lax.optimization_barrier(jnp.sum(dec_in_terms, axis=0))
    grad_dec_out = lax.optimization_barrier(jnp.sum(dec_out_terms, axis=0))
    grad_hyper = lax.optimization_barrier(jnp.sum(hyper_terms_all, axis=0))
    cell_rate = rates.reshape(CELLS) / LATENT
    loss = (jnp.sum(distortions / FEAT + rates / LATENT) / CELLS).reshape(1)
    return (grad_enc_in, grad_enc_out, grad_dec_in, grad_dec_out, grad_hyper, cell_rate, loss)
```

```python
import math

import jax
import jax.numpy as jnp
from jax import lax
from jax.sharding import PartitionSpec as P

LATENT = 64
EDGE = 128

BF = jnp.bfloat16
F32 = jnp.float32
scale_offset = 0.1


def mm(left, right):
    return jnp.dot(left, right, preferred_element_type=F32)


def mm_rows(left, right):
    return lax.dot_general(left, right, (((0,), (0,)), ((), ())), preferred_element_type=F32)


def mm_cells(left, right):
    return lax.dot_general(left, right, (((1,), (1,)), ((), ())), preferred_element_type=F32)


def silu_slope(preact):
    squash = jax.nn.sigmoid(preact)
    return squash * (1.0 + preact * (1.0 - squash))


def shift(block, axis, step):
    count = lax.axis_size(axis)
    return lax.ppermute(block, axis, [(i, (i + step) % count) for i in range(count)])


def swap(block, axis, bit):
    count = lax.axis_size(axis)
    return lax.ppermute(block, axis, [(i, i ^ bit) for i in range(count)])


def pick(block, index, dim):
    return lax.dynamic_index_in_dim(block, index, dim, keepdims=False)


def sum_rows(block):
    n_h, n_l = lax.axis_size("horiz"), lax.axis_size("level")
    n_y = n_h // 2
    me_h, me_l = lax.axis_index("horiz"), lax.axis_index("level")
    core, me_y = me_h % 2, me_h // 2
    rows = block.shape[0] // (n_h * n_l)
    block = block.reshape(n_y, 2, n_l, rows, block.shape[1])
    other = swap(pick(block, 1 - core, 1).astype(BF), "horiz", 1)
    block = pick(block, core, 1).astype(F32) + other.astype(F32)
    got = [
        shift(pick(block, (me_y + d) % n_y, 0).astype(BF), "horiz", 2 * d) for d in range(1, n_y)
    ]
    block = pick(block, me_y, 0)
    for piece in got:
        block = block + piece.astype(F32)
    got = [shift(pick(block, (me_l + d) % n_l, 0).astype(BF), "level", d) for d in range(1, n_l)]
    block = pick(block, me_l, 0)
    for piece in got:
        block = block + piece.astype(F32)
    return block


def sum_all(block):
    n_h, n_l = lax.axis_size("horiz"), lax.axis_size("level")
    bit = 1
    while bit < n_h:
        block = block + swap(block, "horiz", bit)
        bit *= 2
    bit = 1
    while bit < n_l:
        block = block + swap(block, "level", bit)
        bit *= 2
    return block


def sum_halves(block):
    n_h, n_l = lax.axis_size("horiz"), lax.axis_size("level")
    core = lax.axis_index("horiz") % 2
    half = block.shape[1] // 2
    low, high = block[:, :half], block[:, half:]
    first = core == 0
    part = jnp.where(first, low, high) + swap(jnp.where(first, high, low), "horiz", 1)
    bit = 2
    while bit < n_h:
        part = part + swap(part, "horiz", bit)
        bit *= 2
    bit = 1
    while bit < n_l:
        part = part + swap(part, "level", bit)
        bit *= 2
    other = swap(part, "horiz", 1)
    return jnp.concatenate([jnp.where(first, part, other), jnp.where(first, other, part)], axis=1)


def local(fields, enc_in, enc_out, dec_in, dec_out, hyper_weight, neighbours, edge_rows):
    n_h, n_l = lax.axis_size("horiz"), lax.axis_size("level")
    me_l = lax.axis_index("level")
    n_vars, n_lev, part = fields.shape
    cells = part // n_l
    slab = n_vars * n_lev
    feat = slab * n_l
    grad_scale = 1.0 / math.sqrt(part * n_h)

    stored = jnp.transpose(fields, (1, 0, 2)).reshape(slab, part)

    def slab_for(d):
        return lax.dynamic_slice(stored, (0, ((me_l + d) % n_l) * cells), (slab, cells))

    raw = jnp.concatenate(
        [slab_for(0)] + [shift(slab_for(d), "level", d) for d in range(1, n_l)], axis=0
    )
    place = jnp.arange(feat, dtype=jnp.int32)
    source = (me_l - place // slab) % n_l
    target = (place % n_vars) * (n_lev * n_l) + source * n_lev + (place % slab) // n_vars
    order = (place[:, None] == target[None, :]).astype(BF)

    owner = neighbours // cells
    moved = ((me_l - owner) % n_l) * cells + neighbours % cells
    moved = jnp.where(neighbours < part, moved, neighbours)
    limit = part + 2 * EDGE
    entry = lax.broadcasted_iota(jnp.int32, (limit, 1), 0)
    counts = jnp.zeros((limit, cells), F32)
    for k in range(6):
        counts = counts + (moved[k][None, :] == entry).astype(F32)
    counts = counts.astype(BF)
    valid = jnp.sum((neighbours < limit).astype(F32), axis=0)
    mine = lax.broadcasted_iota(jnp.int32, (cells, 1), 0) + me_l * cells
    listed = (edge_rows[0].reshape(1, 2 * EDGE) == mine).astype(BF)

    pre_enc = mm(mm(enc_in, order).astype(BF), raw)
    hidden_enc = jax.nn.silu(pre_enc).astype(BF)
    latent = mm_rows(enc_out, hidden_enc).astype(BF)

    table = [latent] + [shift(latent, "level", d) for d in range(1, n_l)]
    sent = mm(latent, listed).astype(BF)
    halo = jnp.concatenate(
        [shift(sent[:, EDGE:], "horiz", 1), shift(sent[:, :EDGE], "horiz", -1)], axis=1
    )
    halos = [halo] + [shift(halo, "level", d) for d in range(1, n_l)]
    halo = sum(piece.astype(F32) for piece in halos).astype(BF)
    table = jnp.concatenate(table + [halo], axis=1)

    columns = mm(order, raw).astype(BF)
    pre_dec = mm_rows(dec_in, latent)
    hidden_dec = jax.nn.silu(pre_dec).astype(BF)
    recon = mm_rows(dec_out, hidden_dec)
    residual = recon - columns.astype(F32)
    distortion = jnp.sum(residual * residual, axis=0)
    d_recon = (2.0 * grad_scale * residual).astype(BF)
    grad_dec_out = sum_rows(mm_cells(hidden_dec, d_recon))
    d_pre_dec = (mm(dec_out, d_recon) * silu_slope(pre_dec)).astype(BF)
    grad_dec_in = sum_halves(mm_cells(latent, d_pre_dec))
    d_latent = mm(dec_in, d_pre_dec)

    context_b = (mm(table, counts) / valid).astype(BF)
    params = mm_rows(hyper_weight, context_b)
    centre, spread = params[:LATENT], params[LATENT:]
    sigma = scale_offset + jax.nn.softplus(spread)
    scaled = (latent.astype(F32) - centre) / sigma
    rate = jnp.sum(0.5 * scaled * scaled + jnp.log(sigma), axis=0)
    direct = grad_scale * scaled / sigma
    d_spread = grad_scale * (1.0 - scaled * scaled) / sigma * jax.nn.sigmoid(spread)
    d_params = jnp.concatenate([-direct, d_spread], axis=0).astype(BF)
    share = mm(hyper_weight, d_params) / valid
    high = share.astype(BF)
    low = (share - high.astype(F32)).astype(BF)
    both = mm_cells(jnp.concatenate([high, low], axis=0), counts)
    grad_table = both[:LATENT] + both[LATENT:]
    loss_piece = jnp.sum(distortion / feat + rate / LATENT)
    small = sum_all(
        jnp.concatenate(
            [mm_cells(context_b, d_params), jnp.full((8, 2 * LATENT), loss_piece, F32)], axis=0
        )
    )
    grad_hyper = small[:LATENT]
    loss = (small[LATENT, :1] / (part * n_h)).reshape(1)

    back = grad_table[:, part:].astype(BF)
    back = jnp.concatenate(
        [shift(back[:, EDGE:], "horiz", 1), shift(back[:, :EDGE], "horiz", -1)], axis=1
    )
    backs = [back] + [shift(back, "level", d) for d in range(1, n_l)]
    own = grad_table[:, :part]
    got = [
        shift(own[:, d * cells : (d + 1) * cells].astype(BF), "level", -d) for d in range(1, n_l)
    ]
    d_neighbour = own[:, :cells]
    for piece in got:
        d_neighbour = d_neighbour + piece.astype(F32)
    back = sum(piece.astype(F32) for piece in backs)
    high = back.astype(BF)
    low = (back - high.astype(F32)).astype(BF)
    both = mm_cells(jnp.concatenate([high, low], axis=0), listed)
    d_neighbour = d_neighbour + both[:LATENT] + both[LATENT:]
    d_total = (d_latent + direct + d_neighbour).astype(BF)

    grad_enc_out = sum_halves(mm_cells(d_total, hidden_enc)).T
    d_pre_enc = (mm(enc_out, d_total) * silu_slope(pre_enc)).astype(BF)
    grad_enc_in = sum_rows(mm_cells(d_pre_enc, columns))
    return (
        grad_enc_in,
        grad_enc_out,
        grad_dec_in,
        grad_dec_out,
        grad_hyper,
        rate / LATENT,
        loss,
    )


def solution(mesh):
    in_specs = (
        P(None, "level", ("groups", "horiz")),
        P(),
        P(),
        P(),
        P(),
        P(),
        P(None, ("horiz", "level")),
        P("horiz", None, None),
    )
    out_specs = (
        P(("groups", "horiz", "level"), None),
        P("groups", None),
        P("groups", None),
        P(("groups", "horiz", "level"), None),
        P("groups", None),
        P(("groups", "horiz", "level")),
        P("groups"),
    )
    return jax.shard_map(local, mesh=mesh, in_specs=in_specs, out_specs=out_specs, check_vma=False)
```

```python
import math

import jax
import jax.numpy as jnp
from jax import lax
from jax.sharding import PartitionSpec as P

LATENT = 64
EDGE = 128

BF = jnp.bfloat16
F32 = jnp.float32
scale_offset = 0.1


def mm(left, right):
    return jnp.dot(left, right, preferred_element_type=F32)


def mm_rows(left, right):
    return lax.dot_general(left, right, (((0,), (0,)), ((), ())), preferred_element_type=F32)


def mm_cells(left, right):
    return lax.dot_general(left, right, (((1,), (1,)), ((), ())), preferred_element_type=F32)


def silu_slope(preact):
    squash = jax.nn.sigmoid(preact)
    return squash * (1.0 + preact * (1.0 - squash))


def shift(block, axis, step):
    count = lax.axis_size(axis)
    return lax.ppermute(block, axis, [(i, (i + step) % count) for i in range(count)])


def swap(block, axis, bit):
    count = lax.axis_size(axis)
    return lax.ppermute(block, axis, [(i, i ^ bit) for i in range(count)])


def pick(block, index, dim):
    return lax.dynamic_index_in_dim(block, index, dim, keepdims=False)


def after(value, *others):
    return lax.optimization_barrier((value, *others))[0]


def swap_halves(block, dim):
    core = lax.axis_index("horiz") % 2
    other = swap(pick(block, 1 - core, dim).astype(BF), "horiz", 1)
    return pick(block, core, dim).astype(F32) + other.astype(F32)


def to_rows_y(far):
    return [shift(piece.astype(BF), "horiz", 2 * (d + 1)) for d, piece in enumerate(far)]


def to_level(block):
    n_l, me_l = lax.axis_size("level"), lax.axis_index("level")
    return [shift(pick(block, (me_l + d) % n_l, 0).astype(BF), "level", d) for d in range(1, n_l)]


def own_level(block, got):
    block = pick(block, lax.axis_index("level"), 0)
    for piece in got:
        block = block + piece.astype(F32)
    return block


def core_half(rows, product):
    half = rows.shape[0] // 2
    core = lax.axis_index("horiz") % 2
    mine = lax.dynamic_slice_in_dim(rows, core * half, half, 0)
    theirs = lax.dynamic_slice_in_dim(rows, (1 - core) * half, half, 0)
    return product(mine) + swap(product(theirs), "horiz", 1)


def both_halves(part):
    first = lax.axis_index("horiz") % 2 == 0
    other = swap(part, "horiz", 1)
    return jnp.concatenate([jnp.where(first, part, other), jnp.where(first, other, part)], axis=1)


def sum_pairs(part, axis, first, last, kind=F32):
    bit = first
    while bit < last:
        part = part.astype(kind)
        part = part.astype(F32) + swap(part, axis, bit).astype(F32)
        bit *= 2
    return part


def sum_pairs_split(part, axis, first, last):
    bit = first
    while bit < last:
        high = part.astype(BF)
        low = (part[:, -EDGE:] - high[:, -EDGE:].astype(F32)).astype(BF)
        mine = jnp.concatenate([high, low], axis=1)
        mine = mine.astype(F32) + swap(mine, axis, bit).astype(F32)
        part = mine[:, :-EDGE]
        part = jnp.concatenate([part[:, :-EDGE], part[:, -EDGE:] + mine[:, -EDGE:]], axis=1)
        bit *= 2
    return part


def local(fields, enc_in, enc_out, dec_in, dec_out, hyper_weight, neighbours, edge_rows):
    n_h, n_l = lax.axis_size("horiz"), lax.axis_size("level")
    n_y = n_h // 2
    me_l = lax.axis_index("level")
    me_y = lax.axis_index("horiz") // 2
    n_vars, n_lev, part = fields.shape
    cells = part // n_l
    slab = n_vars * n_lev
    feat = slab * n_l
    hidden = enc_in.shape[0]
    grad_scale = 1.0 / math.sqrt(part * n_h)

    stored = jnp.transpose(fields, (1, 0, 2)).reshape(slab, part)

    def slab_for(d):
        return lax.dynamic_slice(stored, (0, ((me_l + d) % n_l) * cells), (slab, cells))

    raw = jnp.concatenate(
        [slab_for(0)] + [shift(slab_for(d), "level", d) for d in range(1, n_l)], axis=0
    )
    place = jnp.arange(feat, dtype=jnp.int32)
    source = (me_l - place // slab) % n_l
    target = (place % n_vars) * (n_lev * n_l) + source * n_lev + (place % slab) // n_vars
    order = (place[:, None] == target[None, :]).astype(BF)

    def relative(position):
        return ((me_l - position // cells) % n_l) * cells + position % cells

    moved = jnp.where(neighbours < part, relative(neighbours), neighbours)
    limit = part + 2 * EDGE
    entry = lax.broadcasted_iota(jnp.int32, (limit, 1), 0)
    counts = jnp.zeros((limit, cells), F32)
    for k in range(6):
        counts = counts + (moved[k][None, :] == entry).astype(F32)
    counts = counts.astype(BF)
    valid = jnp.sum((neighbours < limit).astype(F32), axis=0)
    listed = (relative(edge_rows[0].reshape(1, 2 * EDGE)) == entry[:part]).astype(BF)
    placed = mm(enc_in, order).astype(BF)
    raw, counts, valid, listed, placed, order = lax.optimization_barrier(
        (raw, counts, valid, listed, placed, order)
    )

    pre_enc = mm(placed, raw)
    hidden_enc = jax.nn.silu(pre_enc).astype(BF)
    latent = mm_rows(enc_out, hidden_enc).astype(BF)

    table = jnp.concatenate(
        [latent] + [shift(latent, "level", d) for d in range(1, n_l)], axis=1
    )

    columns = mm(order, raw).astype(BF)
    pre_dec = mm_rows(dec_in, latent)
    hidden_dec = jax.nn.silu(pre_dec).astype(BF)
    residual = mm_rows(dec_out, hidden_dec) - columns.astype(F32)
    distortion = jnp.sum(residual * residual, axis=0)
    d_recon = (2.0 * grad_scale * residual).astype(BF)
    term = mm_cells(hidden_dec, d_recon).reshape(n_y, 2, n_l, hidden // (n_h * n_l), feat)
    term = swap_halves(term, 1)
    d_pre_dec = (mm(dec_out, d_recon) * silu_slope(pre_dec)).astype(BF)
    d_latent = mm(dec_in, d_pre_dec)
    table, d_latent, d_pre_dec, term = lax.optimization_barrier((table, d_latent, d_pre_dec, term))

    sent = mm(table, listed).astype(BF)
    halo = jnp.concatenate(
        [shift(sent[:, EDGE:], "horiz", 1), shift(sent[:, :EDGE], "horiz", -1)], axis=1
    )
    total = mm(table, counts[:part])
    halo, total = lax.optimization_barrier((halo, total))
    total = total + mm(halo, counts[part:])
    context_b = (total / valid).astype(BF)
    params = mm_rows(hyper_weight, context_b)
    centre, spread = params[:LATENT], params[LATENT:]
    sigma = scale_offset + jax.nn.softplus(spread)
    scaled = (latent.astype(F32) - centre) / sigma
    rate = jnp.sum(0.5 * scaled * scaled + jnp.log(sigma), axis=0)
    direct = grad_scale * scaled / sigma
    d_spread = grad_scale * (1.0 - scaled * scaled) / sigma * jax.nn.sigmoid(spread)
    d_params = jnp.concatenate([-direct, d_spread], axis=0).astype(BF)
    share = mm(hyper_weight, d_params) / valid
    high = share.astype(BF)
    low = (share - high.astype(F32)).astype(BF)
    share = jnp.concatenate([high, low], axis=0)

    both = mm_cells(share, counts[part:])
    back = (both[:LATENT] + both[LATENT:]).astype(BF)
    to_next, to_prev = back[:, EDGE:], back[:, :EDGE]
    back = jnp.concatenate([shift(to_next, "horiz", 1), shift(to_prev, "horiz", -1)], axis=1)
    both = mm_cells(after(share, to_next, to_prev), counts[:part])
    back, both = lax.optimization_barrier((back, both))
    own = both[:LATENT] + both[LATENT:] + mm_cells(back, listed)
    got = [
        shift(own[:, d * cells : (d + 1) * cells].astype(BF), "level", -d) for d in range(1, n_l)
    ]
    d_neighbour = own[:, :cells]
    for piece in got:
        d_neighbour = d_neighbour + piece.astype(F32)

    context_b, cell_loss, d_pre_dec, term = lax.optimization_barrier(
        (context_b, distortion / feat + rate / LATENT, d_pre_dec, term, got[0])
    )[:4]
    half_dec = core_half(d_pre_dec, lambda rows: mm_cells(latent, rows))
    small = jnp.concatenate(
        [
            mm_cells(context_b, d_params),
            jnp.pad(cell_loss.reshape(-1, EDGE), ((0, LATENT - cells // EDGE), (0, 0))),
        ],
        axis=1,
    )
    small = small + swap(small, "horiz", 1)
    near_dec = pick(term, me_y, 0)
    far_dec = to_rows_y([pick(term, (me_y + d) % n_y, 0) for d in range(1, n_y)])
    half_dec = sum_pairs(half_dec, "horiz", 2, n_h)
    dec_other = swap(half_dec, "level", 1)
    d_total = (d_latent + direct + d_neighbour).astype(BF)

    core = lax.axis_index("horiz") % 2
    rows = hidden // n_h

    def enc_rows(step, side):
        start = (((me_y + step) % n_y) * 2 + side) * rows
        weight = lax.dynamic_slice(enc_out, (start, 0), (rows, LATENT))
        preact = lax.dynamic_slice(pre_enc, (start, 0), (rows, cells))
        d_pre = lax.optimization_barrier((mm(weight, d_total) * silu_slope(preact)).astype(BF))
        return mm_cells(d_pre, columns)

    def enc_block(step):
        other = enc_rows(step, 1 - core).astype(BF)
        other = swap(other, "horiz", 1)
        kept = enc_rows(step, core)
        return (kept + other.astype(F32)).reshape(n_l, rows // n_l, feat)

    half_enc = core_half(hidden_enc, lambda rows: mm_cells(d_total, rows))
    small = jnp.concatenate([half_enc, small], axis=1)
    small = sum_pairs_split(small, "level", 1, 2)
    sent = [enc_block(d) for d in range(1, n_y)]
    sent, small = lax.optimization_barrier((sent, small))
    arrived = to_rows_y(sent)
    near_dec, half_dec, dec_other = lax.optimization_barrier(
        (near_dec, half_dec, dec_other, *sent)
    )[:3]
    for piece in far_dec:
        near_dec = near_dec + piece.astype(F32)
    got_dec = to_level(near_dec)
    small = sum_pairs_split(small, "level", 2, n_l)
    half_dec = sum_pairs(half_dec + dec_other, "level", 2, n_l, BF)
    near = enc_block(0)
    for piece in arrived:
        near = near + piece.astype(F32)
    near, small, half_dec, near_dec, *got_dec = lax.optimization_barrier(
        (near, small, half_dec, near_dec, *got_dec)
    )
    got_enc = to_level(near)
    small = sum_pairs(small, "horiz", 2, n_h)
    grad_dec_in = both_halves(half_dec)
    width = hidden // 2
    grad_hyper = small[:, width : width + 2 * LATENT]
    loss = (jnp.sum(small[:, width + 2 * LATENT :]) / (part * n_h)).reshape(1)
    grad_dec_out = own_level(near_dec, got_dec)
    grad_enc_out = both_halves(small[:, :width]).T
    grad_enc_in = own_level(near, got_enc)
    return (
        grad_enc_in,
        grad_enc_out,
        grad_dec_in,
        grad_dec_out,
        grad_hyper,
        rate / LATENT,
        loss,
    )


def solution(mesh):
    in_specs = (
        P(None, "level", ("groups", "horiz")),
        P(),
        P(),
        P(),
        P(),
        P(),
        P(None, ("horiz", "level")),
        P("horiz", None, None),
    )
    out_specs = (
        P(("groups", "horiz", "level"), None),
        P("groups", None),
        P("groups", None),
        P(("groups", "horiz", "level"), None),
        P("groups", None),
        P(("groups", "horiz", "level")),
        P("groups"),
    )
    return jax.shard_map(local, mesh=mesh, in_specs=in_specs, out_specs=out_specs, check_vma=False)
```

```python
import math

import jax
import jax.numpy as jnp
from jax import lax
from jax.sharding import PartitionSpec as P

LATENT = 64
EDGE = 128

BF = jnp.bfloat16
F32 = jnp.float32
scale_offset = 0.1


def mm(left, right):
    return jnp.dot(left, right, preferred_element_type=F32)


def mm_rows(left, right):
    return lax.dot_general(left, right, (((0,), (0,)), ((), ())), preferred_element_type=F32)


def mm_cells(left, right):
    return lax.dot_general(left, right, (((1,), (1,)), ((), ())), preferred_element_type=F32)


def silu_slope(preact):
    squash = jax.nn.sigmoid(preact)
    return squash * (1.0 + preact * (1.0 - squash))


def shift(block, axis, step):
    count = lax.axis_size(axis)
    return lax.ppermute(block, axis, [(i, (i + step) % count) for i in range(count)])


def swap(block, axis, bit):
    count = lax.axis_size(axis)
    return lax.ppermute(block, axis, [(i, i ^ bit) for i in range(count)])


def pick(block, index, dim):
    return lax.dynamic_index_in_dim(block, index, dim, keepdims=False)


def after(value, *others):
    return lax.optimization_barrier((value, *others))[0]


def swap_halves(block, dim):
    core = lax.axis_index("horiz") % 2
    other = swap(pick(block, 1 - core, dim).astype(BF), "horiz", 1)
    return pick(block, core, dim).astype(F32) + other.astype(F32)


def to_rows_y(far):
    return [shift(piece.astype(BF), "horiz", 2 * (d + 1)) for d, piece in enumerate(far)]


def sum_y(pieces):
    count = len(pieces)
    pieces = [piece.astype(F32) for piece in pieces]
    if count > 2:
        me_y = lax.axis_index("horiz") // 2
        stacked = jnp.stack(pieces)
        pieces = [pick(stacked, (me_y - y) % count, 0) for y in range(count)]
    return sum(pieces)


def to_level(block):
    n_l, me_l = lax.axis_size("level"), lax.axis_index("level")
    return [shift(pick(block, (me_l + d) % n_l, 0).astype(BF), "level", d) for d in range(1, n_l)]


def own_level(block, got):
    block = pick(block, lax.axis_index("level"), 0)
    for piece in got:
        block = block + piece.astype(F32)
    return block


def halves(rows, product):
    half = rows.shape[0] // 2
    core = lax.axis_index("horiz") % 2
    mine = lax.dynamic_slice_in_dim(rows, core * half, half, 0)
    theirs = lax.dynamic_slice_in_dim(rows, (1 - core) * half, half, 0)
    return product(mine), product(theirs)


def both_halves(part):
    first = lax.axis_index("horiz") % 2 == 0
    other = swap(part, "horiz", 1)
    return jnp.concatenate([jnp.where(first, part, other), jnp.where(first, other, part)], axis=1)


def pack(block, extra):
    high = extra.astype(BF)
    low = (extra - high.astype(F32)).astype(BF)
    both = jnp.concatenate([high, low], axis=0)
    both = jnp.pad(both, ((0, 0), (0, block.shape[1] - both.shape[1])))
    return jnp.concatenate([block.astype(BF), both], axis=0)


def unpack(packed, rows, high):
    packed = packed.astype(F32)
    extra = packed[rows:, :EDGE]
    return packed[:rows], extra[:high] + extra[high:]


def tree(pieces):
    while len(pieces) > 1:
        pieces = [a + b for a, b in zip(pieces[::2], pieces[1::2])]
    return pieces[0]


def local(fields, enc_in, enc_out, dec_in, dec_out, hyper_weight, neighbours, edge_rows):
    n_h, n_l = lax.axis_size("horiz"), lax.axis_size("level")
    n_y = n_h // 2
    me_l = lax.axis_index("level")
    me_y = lax.axis_index("horiz") // 2
    n_vars, n_lev, part = fields.shape
    cells = part // n_l
    slab = n_vars * n_lev
    feat = slab * n_l
    hidden = enc_in.shape[0]
    grad_scale = 1.0 / math.sqrt(part * n_h)

    stored = jnp.transpose(fields, (1, 0, 2)).reshape(slab, part)

    def slab_for(d):
        return lax.dynamic_slice(stored, (0, ((me_l + d) % n_l) * cells), (slab, cells))

    raw = jnp.concatenate(
        [slab_for(0)] + [shift(slab_for(d), "level", d) for d in range(1, n_l)], axis=0
    )
    place = jnp.arange(feat, dtype=jnp.int32)
    source = (me_l - place // slab) % n_l
    target = (place % n_vars) * (n_lev * n_l) + source * n_lev + (place % slab) // n_vars
    order = (place[:, None] == target[None, :]).astype(BF)

    def relative(position):
        return ((me_l - position // cells) % n_l) * cells + position % cells

    moved = jnp.where(neighbours < part, relative(neighbours), neighbours)
    limit = part + 2 * EDGE
    entry = lax.broadcasted_iota(jnp.int32, (limit, 1), 0)
    counts = jnp.zeros((limit, cells), F32)
    for k in range(6):
        counts = counts + (moved[k][None, :] == entry).astype(F32)
    counts = counts.astype(BF)
    valid = jnp.sum((neighbours < limit).astype(F32), axis=0)
    listed = (relative(edge_rows[0].reshape(1, 2 * EDGE)) == entry[:part]).astype(BF)
    placed = mm(enc_in, order).astype(BF)
    raw, counts, valid, listed, placed, order = lax.optimization_barrier(
        (raw, counts, valid, listed, placed, order)
    )

    pre_enc = mm(placed, raw)
    hidden_enc = jax.nn.silu(pre_enc).astype(BF)
    latent = mm_rows(enc_out, hidden_enc).astype(BF)

    table = jnp.concatenate(
        [latent] + [shift(latent, "level", d) for d in range(1, n_l)], axis=1
    )

    columns = mm(order, raw).astype(BF)
    pre_dec = mm_rows(dec_in, latent)
    hidden_dec = jax.nn.silu(pre_dec).astype(BF)
    residual = mm_rows(dec_out, hidden_dec) - columns.astype(F32)
    distortion = jnp.sum(residual * residual, axis=0)
    d_recon = (2.0 * grad_scale * residual).astype(BF)
    term = mm_cells(hidden_dec, d_recon).reshape(n_y, 2, n_l, hidden // (n_h * n_l), feat)
    term = swap_halves(term, 1)
    d_pre_dec = (mm(dec_out, d_recon) * silu_slope(pre_dec)).astype(BF)
    d_latent = mm(dec_in, d_pre_dec)
    half_dec = halves(d_pre_dec, lambda rows: mm_cells(latent, rows))
    table, d_latent, half_dec, term = lax.optimization_barrier((table, d_latent, half_dec, term))

    sent = mm(table, listed).astype(BF)
    halo = jnp.concatenate(
        [shift(sent[:, EDGE:], "horiz", 1), shift(sent[:, :EDGE], "horiz", -1)], axis=1
    )
    total = mm(table, counts[:part])
    halo, total = lax.optimization_barrier((halo, total))
    total = total + mm(halo, counts[part:])
    context_b = (total / valid).astype(BF)
    params = mm_rows(hyper_weight, context_b)
    centre, spread = params[:LATENT], params[LATENT:]
    sigma = scale_offset + jax.nn.softplus(spread)
    scaled = (latent.astype(F32) - centre) / sigma
    rate = jnp.sum(0.5 * scaled * scaled + jnp.log(sigma), axis=0)
    direct = grad_scale * scaled / sigma
    d_spread = grad_scale * (1.0 - scaled * scaled) / sigma * jax.nn.sigmoid(spread)
    d_params = jnp.concatenate([-direct, d_spread], axis=0).astype(BF)
    share = mm(hyper_weight, d_params) / valid
    high = share.astype(BF)
    low = (share - high.astype(F32)).astype(BF)
    share = jnp.concatenate([high, low], axis=0)

    both = mm_cells(share, counts[part:])
    back = (both[:LATENT] + both[LATENT:]).astype(BF)
    to_next, to_prev = back[:, EDGE:], back[:, :EDGE]
    back = jnp.concatenate([shift(to_next, "horiz", 1), shift(to_prev, "horiz", -1)], axis=1)
    both = mm_cells(after(share, to_next, to_prev), counts[:part])
    back, both = lax.optimization_barrier((back, both))
    own = both[:LATENT] + both[LATENT:] + mm_cells(back, listed)
    got = [
        shift(own[:, d * cells : (d + 1) * cells].astype(BF), "level", -d) for d in range(1, n_l)
    ]
    d_neighbour = own[:, :cells]
    for piece in got:
        d_neighbour = d_neighbour + piece.astype(F32)

    core = lax.axis_index("horiz") % 2
    rows = hidden // n_h
    width = hidden // 2
    term, half_dec = lax.optimization_barrier((term, half_dec, own))[:2]
    half_dec = (half_dec[0] + swap(half_dec[1], "horiz", 1)).astype(BF)
    rider = jnp.pad(half_dec, ((0, 0), (0, feat - width)))
    near_dec = pick(term, me_y, 0)
    far = [pick(term, (me_y + d) % n_y, 0).reshape(rows, feat) for d in range(1, n_y)]
    far = to_rows_y([jnp.concatenate([piece.astype(BF), rider], axis=0) for piece in far])
    context_b, cell_loss = lax.optimization_barrier(
        (context_b, distortion / feat + rate / LATENT, got[0])
    )[:2]
    hyper = mm_cells(context_b, d_params)
    hyper = hyper + swap(hyper, "horiz", 1)
    cell_loss = cell_loss.reshape(-1, EDGE)
    cell_loss = cell_loss + swap(cell_loss, "horiz", 1)
    high = cell_loss.shape[0]
    d_total = (d_latent + direct + d_neighbour).astype(BF)
    d_total, hyper, cell_loss, *far = lax.optimization_barrier((d_total, hyper, cell_loss, *far))

    half_enc = halves(hidden_enc, lambda block: mm_cells(d_total, block))
    half_enc = half_enc[0] + swap(half_enc[1], "horiz", 1)

    def enc_rows(side):
        weight = pick(enc_out.reshape(n_y, 2, rows, LATENT), side, 1).reshape(n_y * rows, LATENT)
        preact = pick(pre_enc.reshape(n_y, 2, rows, cells), side, 1).reshape(n_y * rows, cells)
        d_pre = lax.optimization_barrier((mm(weight, d_total) * silu_slope(preact)).astype(BF))
        return mm_cells(d_pre, columns)

    other = swap(enc_rows(1 - core).astype(BF), "horiz", 1)
    near = (enc_rows(core) + other.astype(F32)).reshape(n_y, rows, feat)
    rider = pack(jnp.concatenate([half_enc, hyper], axis=1), cell_loss)
    sent = [pick(near, (me_y + d) % n_y, 0).astype(BF) for d in range(1, n_y)]
    sent = [jnp.concatenate([piece, rider], axis=0) for piece in sent]
    for piece in far:
        near_dec = near_dec + piece[:rows].reshape(near_dec.shape).astype(F32)
    half_dec = sum_y([half_dec] + [piece[rows:, :width] for piece in far]).astype(BF)
    near, near_dec, half_dec, sent = lax.optimization_barrier(
        (pick(near, me_y, 0), near_dec, half_dec, sent)
    )

    arrived = to_rows_y(sent)
    got_dec = [
        swap(
            jnp.concatenate(
                [pick(near_dec, me_l ^ d, 0).astype(BF).reshape(LATENT, -1), half_dec], axis=1
            ),
            "level",
            d,
        )
        for d in range(1, n_l)
    ]
    near, arrived, got_dec = lax.optimization_barrier((near, arrived, got_dec))

    for piece in arrived:
        near = near + piece[:rows].astype(F32)
    near = near.reshape(n_l, rows // n_l, feat)
    riders = [rider] + [piece[rows:] for piece in arrived]
    riders = [unpack(piece, LATENT, high) for piece in riders]
    rider = pack(*(sum_y(list(pieces)) for pieces in zip(*riders)))
    got_enc = [
        swap(jnp.concatenate([pick(near, me_l ^ d, 0).astype(BF), rider], axis=0), "level", d)
        for d in range(1, n_l)
    ]
    few = rows // n_l
    riders = [unpack(piece, LATENT, high) for piece in [rider] + [p[few:] for p in got_enc]]
    half_enc, cell_loss = (tree(list(pieces)) for pieces in zip(*riders))
    grad_dec_out = pick(near_dec, me_l, 0)
    for piece in got_dec:
        piece = piece[:, :-width].reshape(grad_dec_out.shape)
        grad_dec_out = grad_dec_out + piece.astype(F32)
    half_dec = tree([half_dec.astype(F32)] + [piece[:, -width:].astype(F32) for piece in got_dec])
    grad_dec_in = both_halves(half_dec)
    grad_hyper = half_enc[:, width:]
    loss = (jnp.sum(cell_loss) / (part * n_h)).reshape(1)
    grad_enc_out = both_halves(half_enc[:, :width]).T
    grad_enc_in = pick(near, me_l, 0)
    for piece in got_enc:
        grad_enc_in = grad_enc_in + piece[:few].astype(F32)
    return (
        grad_enc_in,
        grad_enc_out,
        grad_dec_in,
        grad_dec_out,
        grad_hyper,
        rate / LATENT,
        loss,
    )


def solution(mesh):
    in_specs = (
        P(None, "level", ("groups", "horiz")),
        P(),
        P(),
        P(),
        P(),
        P(),
        P(None, ("horiz", "level")),
        P("horiz", None, None),
    )
    out_specs = (
        P(("groups", "horiz", "level"), None),
        P("groups", None),
        P("groups", None),
        P(("groups", "horiz", "level"), None),
        P("groups", None),
        P(("groups", "horiz", "level")),
        P("groups"),
    )
    return jax.shard_map(local, mesh=mesh, in_specs=in_specs, out_specs=out_specs, check_vma=False)
```

```python
import functools
import math

import jax
import jax.numpy as jnp
from jax import lax
from jax.experimental import pallas as pl
from jax.experimental.pallas import tpu as pltpu
from jax.sharding import PartitionSpec as P

LATENT = 64
EDGE = 128

BF = jnp.bfloat16
F32 = jnp.float32
scale_offset = 0.1


def mm(left, right):
    return jnp.dot(left, right, preferred_element_type=F32)


def mm_rows(left, right):
    return lax.dot_general(left, right, (((0,), (0,)), ((), ())), preferred_element_type=F32)


def mm_cells(left, right):
    return lax.dot_general(left, right, (((1,), (1,)), ((), ())), preferred_element_type=F32)


def silu_slope(preact):
    squash = jax.nn.sigmoid(preact)
    return squash * (1.0 + preact * (1.0 - squash))


def shift(block, axis, step):
    count = lax.axis_size(axis)
    return lax.ppermute(block, axis, [(i, (i + step) % count) for i in range(count)])


def swap(block, axis, bit):
    count = lax.axis_size(axis)
    return lax.ppermute(block, axis, [(i, i ^ bit) for i in range(count)])


def pick(block, index, dim):
    return lax.dynamic_index_in_dim(block, index, dim, keepdims=False)


def after(value, *others):
    return lax.optimization_barrier((value, *others))[0]


def swap_halves(block, dim):
    core = lax.axis_index("horiz") % 2
    other = swap(pick(block, 1 - core, dim).astype(BF), "horiz", 1)
    return pick(block, core, dim).astype(F32) + other.astype(F32)


def to_rows_y(far):
    return [shift(piece.astype(BF), "horiz", 2 * (d + 1)) for d, piece in enumerate(far)]


def sum_y(pieces):
    count = len(pieces)
    pieces = [piece.astype(F32) for piece in pieces]
    if count > 2:
        me_y = lax.axis_index("horiz") // 2
        stacked = jnp.stack(pieces)
        pieces = [pick(stacked, (me_y - y) % count, 0) for y in range(count)]
    return sum(pieces)


def to_level(block):
    n_l, me_l = lax.axis_size("level"), lax.axis_index("level")
    return [shift(pick(block, (me_l + d) % n_l, 0).astype(BF), "level", d) for d in range(1, n_l)]


def own_level(block, got):
    block = pick(block, lax.axis_index("level"), 0)
    for piece in got:
        block = block + piece.astype(F32)
    return block


def halves(rows, product):
    half = rows.shape[0] // 2
    core = lax.axis_index("horiz") % 2
    mine = lax.dynamic_slice_in_dim(rows, core * half, half, 0)
    theirs = lax.dynamic_slice_in_dim(rows, (1 - core) * half, half, 0)
    return product(mine), product(theirs)


def both_halves(part):
    first = lax.axis_index("horiz") % 2 == 0
    other = swap(part, "horiz", 1)
    return jnp.concatenate([jnp.where(first, part, other), jnp.where(first, other, part)], axis=1)


def pack(block, extra):
    high = lax.reduce_precision(extra, 8, 7)
    both = jnp.concatenate([high, extra - high], axis=1).astype(BF)
    both = jnp.pad(both, ((0, 0), (0, block.shape[1] - both.shape[1])))
    return jnp.concatenate([block.astype(BF), both], axis=0)


def unpack(packed, rows):
    packed = packed.astype(F32)
    return packed[:rows], packed[rows:, :EDGE] + packed[rows:, EDGE : 2 * EDGE]


def tree(pieces):
    while len(pieces) > 1:
        pieces = [a + b for a, b in zip(pieces[::2], pieces[1::2])]
    return pieces[0]


def encode_kernel(step, *refs):
    *slab_refs, placed_ref, out_t_ref, raw_ref, pre_ref, hidden_ref, latent_ref = refs
    slab = slab_refs[0].shape[0]
    hidden, cells = pre_ref.shape
    for d, slab_ref in enumerate(slab_refs):
        raw_ref[d * slab : (d + 1) * slab, :] = slab_ref[...]

    latent = jnp.zeros(latent_ref.shape, F32)
    for start in range(0, hidden, step):
        rows = slice(start, start + step)
        preact = jnp.dot(placed_ref[rows, :], raw_ref[...], preferred_element_type=F32)
        pre_ref[rows, :] = preact
        active = (preact * jax.nn.sigmoid(preact)).astype(BF)
        hidden_ref[rows, :] = active
        latent += jnp.dot(out_t_ref[:, rows], active, preferred_element_type=F32)
    latent_ref[...] = latent.astype(BF)


def encode(slabs, placed, out_t):
    slab, cells = slabs[0].shape
    hidden, feat = placed.shape
    vmem = pl.BlockSpec(memory_space=pltpu.VMEM)
    flops = 2 * hidden * cells * (feat + out_t.shape[0])
    size = 4 * hidden * cells + 2 * (hidden * cells + 2 * feat * cells + hidden * feat)
    return pl.pallas_call(
        functools.partial(encode_kernel, hidden // 4),
        out_shape=[
            jax.ShapeDtypeStruct((feat, cells), BF),
            jax.ShapeDtypeStruct((hidden, cells), F32),
            jax.ShapeDtypeStruct((hidden, cells), BF),
            jax.ShapeDtypeStruct((out_t.shape[0], cells), BF),
        ],
        in_specs=[vmem] * (len(slabs) + 2),
        out_specs=[vmem] * 4,
        compiler_params=pltpu.CompilerParams(vmem_limit_bytes=24 * 2**20),
        cost_estimate=pl.CostEstimate(
            flops=flops, bytes_accessed=size, transcendentals=hidden * cells
        ),
    )(*slabs, placed, out_t)


def local(fields, enc_in, enc_out, dec_in, dec_out, hyper_weight, neighbours, edge_rows):
    n_h, n_l = lax.axis_size("horiz"), lax.axis_size("level")
    n_y = n_h // 2
    me_l = lax.axis_index("level")
    me_y = lax.axis_index("horiz") // 2
    n_vars, n_lev, part = fields.shape
    cells = part // n_l
    slab = n_vars * n_lev
    feat = slab * n_l
    hidden = enc_in.shape[0]
    grad_scale = 1.0 / math.sqrt(part * n_h)

    stored = jnp.transpose(fields, (1, 0, 2)).reshape(slab, part)

    def slab_for(d):
        return lax.dynamic_slice(stored, (0, ((me_l + d) % n_l) * cells), (slab, cells))

    slabs = [slab_for(0)] + [shift(slab_for(d), "level", d) for d in range(1, n_l)]
    place = jnp.arange(feat, dtype=jnp.int32)
    source = (me_l - place // slab) % n_l
    target = (place % n_vars) * (n_lev * n_l) + source * n_lev + (place % slab) // n_vars
    order = (place[:, None] == target[None, :]).astype(BF)

    def relative(position):
        return ((me_l - position // cells) % n_l) * cells + position % cells

    moved = jnp.where(neighbours < part, relative(neighbours), neighbours)
    limit = part + 2 * EDGE
    entry = lax.broadcasted_iota(jnp.int32, (limit, 1), 0)
    counts = jnp.zeros((limit, cells), F32)
    for k in range(6):
        counts = counts + (moved[k][None, :] == entry).astype(F32)
    counts = counts.astype(BF)
    valid = jnp.sum((neighbours < limit).astype(F32), axis=0)
    listed = (relative(edge_rows[0].reshape(1, 2 * EDGE)) == entry[:part]).astype(BF)
    placed = mm(enc_in, order).astype(BF)
    slabs, counts, valid, listed, placed, order = lax.optimization_barrier(
        (slabs, counts, valid, listed, placed, order)
    )

    raw, pre_enc, hidden_enc, latent = encode(slabs, placed, enc_out.T)

    table = jnp.concatenate(
        [latent] + [shift(latent, "level", d) for d in range(1, n_l)], axis=1
    )

    columns = mm(order, raw).astype(BF)
    pre_dec = mm_rows(dec_in, latent)
    hidden_dec = jax.nn.silu(pre_dec).astype(BF)
    residual = mm_rows(dec_out, hidden_dec) - columns.astype(F32)
    distortion = jnp.sum(residual * residual, axis=0)
    d_recon = (2.0 * grad_scale * residual).astype(BF)
    term = mm_cells(hidden_dec, d_recon).reshape(n_y, 2, n_l, hidden // (n_h * n_l), feat)
    term = swap_halves(term, 1)
    d_pre_dec = (mm(dec_out, d_recon) * silu_slope(pre_dec)).astype(BF)
    d_latent = mm(dec_in, d_pre_dec)
    half_dec = halves(d_pre_dec, lambda rows: mm_cells(latent, rows))
    table, d_latent, half_dec, term = lax.optimization_barrier((table, d_latent, half_dec, term))

    sent = mm(table, listed).astype(BF)
    halo = jnp.concatenate(
        [shift(sent[:, EDGE:], "horiz", 1), shift(sent[:, :EDGE], "horiz", -1)], axis=1
    )
    total = mm(table, counts[:part])
    halo, total = lax.optimization_barrier((halo, total))
    total = total + mm(halo, counts[part:])
    context_b = (total / valid).astype(BF)
    params = mm_rows(hyper_weight, context_b)
    centre, spread = params[:LATENT], params[LATENT:]
    sigma = scale_offset + jax.nn.softplus(spread)
    scaled = (latent.astype(F32) - centre) / sigma
    rate = jnp.sum(0.5 * scaled * scaled + jnp.log(sigma), axis=0)
    direct = grad_scale * scaled / sigma
    d_spread = grad_scale * (1.0 - scaled * scaled) / sigma * jax.nn.sigmoid(spread)
    d_params = jnp.concatenate([-direct, d_spread], axis=0).astype(BF)
    share = mm(hyper_weight, d_params) / valid
    share = share.astype(BF)

    back = mm_cells(share, counts[part:]).astype(BF)
    to_next, to_prev = back[:, EDGE:], back[:, :EDGE]
    back = jnp.concatenate([shift(to_next, "horiz", 1), shift(to_prev, "horiz", -1)], axis=1)
    own = mm_cells(after(share, to_next, to_prev), counts[:part])
    back, own = lax.optimization_barrier((back, own))
    own = own + mm_cells(back, listed)
    got = [
        shift(own[:, d * cells : (d + 1) * cells].astype(BF), "level", -d) for d in range(1, n_l)
    ]
    d_neighbour = own[:, :cells]
    for piece in got:
        d_neighbour = d_neighbour + piece.astype(F32)

    core = lax.axis_index("horiz") % 2
    rows = hidden // n_h
    width = hidden // 2
    term, half_dec = lax.optimization_barrier((term, half_dec, own))[:2]
    half_dec = (half_dec[0] + swap(half_dec[1], "horiz", 1)).astype(BF)
    rider = jnp.pad(half_dec, ((0, 0), (0, feat - width)))
    near_dec = pick(term, me_y, 0)
    far = [pick(term, (me_y + d) % n_y, 0).reshape(rows, feat) for d in range(1, n_y)]
    far = to_rows_y([jnp.concatenate([piece.astype(BF), rider], axis=0) for piece in far])
    context_b, cell_loss = lax.optimization_barrier(
        (context_b, distortion / feat + rate / LATENT, got[0])
    )[:2]
    hyper = mm_cells(context_b, d_params)
    hyper = hyper + swap(hyper, "horiz", 1)
    cell_loss = cell_loss.reshape(-1, EDGE)
    cell_loss = cell_loss + swap(cell_loss, "horiz", 1)
    d_total = (d_latent + direct + d_neighbour).astype(BF)
    d_total, hyper, cell_loss, *far = lax.optimization_barrier((d_total, hyper, cell_loss, *far))

    half_enc = halves(hidden_enc, lambda block: mm_cells(d_total, block))
    half_enc = half_enc[0] + swap(half_enc[1], "horiz", 1)

    def enc_rows(side):
        weight = pick(enc_out.reshape(n_y, 2, rows, LATENT), side, 1).reshape(n_y * rows, LATENT)
        preact = pick(pre_enc.reshape(n_y, 2, rows, cells), side, 1).reshape(n_y * rows, cells)
        d_pre = lax.optimization_barrier((mm(weight, d_total) * silu_slope(preact)).astype(BF))
        return mm_cells(d_pre, columns)

    other = swap(enc_rows(1 - core).astype(BF), "horiz", 1)
    near = (enc_rows(core) + other.astype(F32)).reshape(n_y, rows, feat)
    rider = pack(jnp.concatenate([half_enc, hyper], axis=1), cell_loss)
    sent = [pick(near, (me_y + d) % n_y, 0).astype(BF) for d in range(1, n_y)]
    sent = [jnp.concatenate([piece, rider], axis=0) for piece in sent]
    for piece in far:
        near_dec = near_dec + piece[:rows].reshape(near_dec.shape).astype(F32)
    half_dec = sum_y([half_dec] + [piece[rows:, :width] for piece in far]).astype(BF)
    near, near_dec, half_dec, sent = lax.optimization_barrier(
        (pick(near, me_y, 0), near_dec, half_dec, sent)
    )

    arrived = to_rows_y(sent)
    got_dec = []
    for d in range(1, n_l):
        piece = pick(near_dec, me_l ^ d, 0).astype(BF).reshape(LATENT, -1)
        got_dec.append(swap(jnp.concatenate([piece] + [half_dec] * (d == 1), axis=1), "level", d))
    near, arrived, got_dec = lax.optimization_barrier((near, arrived, got_dec))

    for piece in arrived:
        near = near + piece[:rows].astype(F32)
    near = near.reshape(n_l, rows // n_l, feat)
    riders = [rider] + [piece[rows:] for piece in arrived]
    riders = [unpack(piece, LATENT) for piece in riders]
    rider = pack(*(sum_y(list(pieces)) for pieces in zip(*riders)))
    span = got_dec[1].shape[1]
    half_dec = (half_dec.astype(F32) + got_dec[0][:, span:].astype(F32)).astype(BF)
    few = rows // n_l
    wide = jnp.pad(half_dec, ((0, 0), (0, feat - width)))
    got_enc = [
        swap(
            jnp.concatenate(
                [pick(near, me_l ^ d, 0).astype(BF), rider] + [wide] * (d == 2), axis=0
            ),
            "level",
            d,
        )
        for d in range(1, n_l)
    ]
    size = few + rider.shape[0]
    half_dec = half_dec.astype(F32) + got_enc[1][size:, :width].astype(F32)
    got_enc = [piece[:size] for piece in got_enc]
    riders = [unpack(piece, LATENT) for piece in [rider] + [p[few:] for p in got_enc]]
    half_enc, cell_loss = (tree(list(pieces)) for pieces in zip(*riders))
    grad_dec_out = pick(near_dec, me_l, 0)
    for piece in got_dec:
        piece = piece[:, :span].reshape(grad_dec_out.shape)
        grad_dec_out = grad_dec_out + piece.astype(F32)
    bit = 4
    while bit < n_l:
        half_dec = half_dec.astype(BF)
        half_dec = half_dec.astype(F32) + swap(half_dec, "level", bit).astype(F32)
        bit *= 2
    grad_dec_in = both_halves(after(half_dec, *got_enc))
    grad_hyper = half_enc[:, width:]
    loss = (jnp.sum(cell_loss) / (part * n_h)).reshape(1)
    grad_enc_out = both_halves(half_enc[:, :width]).T
    grad_enc_in = pick(near, me_l, 0)
    for piece in got_enc:
        grad_enc_in = grad_enc_in + piece[:few].astype(F32)
    return (
        grad_enc_in,
        grad_enc_out,
        grad_dec_in,
        grad_dec_out,
        grad_hyper,
        rate / LATENT,
        loss,
    )


def solution(mesh):
    in_specs = (
        P(None, "level", ("groups", "horiz")),
        P(),
        P(),
        P(),
        P(),
        P(),
        P(None, ("horiz", "level")),
        P("horiz", None, None),
    )
    out_specs = (
        P(("groups", "horiz", "level"), None),
        P("groups", None),
        P("groups", None),
        P(("groups", "horiz", "level"), None),
        P("groups", None),
        P(("groups", "horiz", "level")),
        P("groups"),
    )
    return jax.shard_map(local, mesh=mesh, in_specs=in_specs, out_specs=out_specs, check_vma=False)
```

```python
import functools
import math

import jax
import jax.numpy as jnp
from jax import lax
from jax.experimental import pallas as pl
from jax.experimental.pallas import tpu as pltpu
from jax.sharding import PartitionSpec as P

LATENT = 64
EDGE = 128

BF = jnp.bfloat16
F32 = jnp.float32
scale_offset = 0.1


def mm(left, right):
    return jnp.dot(left, right, preferred_element_type=F32)


def mm_rows(left, right):
    return lax.dot_general(left, right, (((0,), (0,)), ((), ())), preferred_element_type=F32)


def mm_cells(left, right):
    return lax.dot_general(left, right, (((1,), (1,)), ((), ())), preferred_element_type=F32)


def silu_slope(preact):
    squash = jax.nn.sigmoid(preact)
    return squash * (1.0 + preact * (1.0 - squash))


def shift(block, axis, step):
    count = lax.axis_size(axis)
    return lax.ppermute(block, axis, [(i, (i + step) % count) for i in range(count)])


def swap(block, axis, bit):
    count = lax.axis_size(axis)
    return lax.ppermute(block, axis, [(i, i ^ bit) for i in range(count)])


def pick(block, index, dim):
    return lax.dynamic_index_in_dim(block, index, dim, keepdims=False)


def after(value, *others):
    return lax.optimization_barrier((value, *others))[0]


def swap_halves(block, dim):
    core = lax.axis_index("horiz") % 2
    other = swap(pick(block, 1 - core, dim).astype(BF), "horiz", 1)
    return pick(block, core, dim).astype(F32) + other.astype(F32)


def to_rows_y(far):
    return [shift(piece.astype(BF), "horiz", 2 * (d + 1)) for d, piece in enumerate(far)]


def sum_y(pieces):
    count = len(pieces)
    pieces = [piece.astype(F32) for piece in pieces]
    if count > 2:
        me_y = lax.axis_index("horiz") // 2
        stacked = jnp.stack(pieces)
        pieces = [pick(stacked, (me_y - y) % count, 0) for y in range(count)]
    return sum(pieces)


def to_level(block):
    n_l, me_l = lax.axis_size("level"), lax.axis_index("level")
    return [shift(pick(block, (me_l + d) % n_l, 0).astype(BF), "level", d) for d in range(1, n_l)]


def own_level(block, got):
    block = pick(block, lax.axis_index("level"), 0)
    for piece in got:
        block = block + piece.astype(F32)
    return block


def halves(rows, product):
    half = rows.shape[0] // 2
    core = lax.axis_index("horiz") % 2
    mine = lax.dynamic_slice_in_dim(rows, core * half, half, 0)
    theirs = lax.dynamic_slice_in_dim(rows, (1 - core) * half, half, 0)
    return product(mine), product(theirs)


def both_halves(part):
    first = lax.axis_index("horiz") % 2 == 0
    other = swap(part, "horiz", 1)
    return jnp.concatenate([jnp.where(first, part, other), jnp.where(first, other, part)], axis=1)


def pack(block, extra):
    high = lax.reduce_precision(extra, 8, 7)
    both = jnp.concatenate([high, extra - high], axis=1).astype(BF)
    both = jnp.pad(both, ((0, 0), (0, block.shape[1] - both.shape[1])))
    return jnp.concatenate([block.astype(BF), both], axis=0)


def unpack(packed, rows):
    packed = packed.astype(F32)
    return packed[:rows], packed[rows:, :EDGE] + packed[rows:, EDGE : 2 * EDGE]


def sum_pairs(part, axis, first, last, kind):
    bit = first
    while bit < last:
        part = part.astype(kind)
        part = part.astype(F32) + swap(part, axis, bit).astype(F32)
        bit *= 2
    return part


def tree(pieces):
    while len(pieces) > 1:
        pieces = [a + b for a, b in zip(pieces[::2], pieces[1::2])]
    return pieces[0]


def encode_kernel(step, *refs):
    *slab_refs, placed_ref, out_t_ref, raw_ref, pre_ref, hidden_ref, latent_ref = refs
    slab = slab_refs[0].shape[0]
    hidden, cells = pre_ref.shape
    for d, slab_ref in enumerate(slab_refs):
        raw_ref[d * slab : (d + 1) * slab, :] = slab_ref[...]

    latent = jnp.zeros(latent_ref.shape, F32)
    for start in range(0, hidden, step):
        rows = slice(start, start + step)
        preact = jnp.dot(placed_ref[rows, :], raw_ref[...], preferred_element_type=F32)
        pre_ref[rows, :] = preact
        active = (preact * jax.nn.sigmoid(preact)).astype(BF)
        hidden_ref[rows, :] = active
        latent += jnp.dot(out_t_ref[:, rows], active, preferred_element_type=F32)
    latent_ref[...] = latent.astype(BF)


def encode(slabs, placed, out_t):
    slab, cells = slabs[0].shape
    hidden, feat = placed.shape
    vmem = pl.BlockSpec(memory_space=pltpu.VMEM)
    flops = 2 * hidden * cells * (feat + out_t.shape[0])
    size = 4 * hidden * cells + 2 * (hidden * cells + 2 * feat * cells + hidden * feat)
    return pl.pallas_call(
        functools.partial(encode_kernel, hidden // 4),
        out_shape=[
            jax.ShapeDtypeStruct((feat, cells), BF),
            jax.ShapeDtypeStruct((hidden, cells), F32),
            jax.ShapeDtypeStruct((hidden, cells), BF),
            jax.ShapeDtypeStruct((out_t.shape[0], cells), BF),
        ],
        in_specs=[vmem] * (len(slabs) + 2),
        out_specs=[vmem] * 4,
        compiler_params=pltpu.CompilerParams(vmem_limit_bytes=24 * 2**20),
        cost_estimate=pl.CostEstimate(
            flops=flops, bytes_accessed=size, transcendentals=hidden * cells
        ),
    )(*slabs, placed, out_t)


def local(fields, enc_in, enc_out, dec_in, dec_out, hyper_weight, neighbours, edge_rows):
    n_h, n_l = lax.axis_size("horiz"), lax.axis_size("level")
    n_y = n_h // 2
    me_l = lax.axis_index("level")
    me_y = lax.axis_index("horiz") // 2
    n_vars, n_lev, part = fields.shape
    cells = part // n_l
    slab = n_vars * n_lev
    feat = slab * n_l
    hidden = enc_in.shape[0]
    grad_scale = 1.0 / math.sqrt(part * n_h)

    stored = jnp.transpose(fields, (1, 0, 2)).reshape(slab, part)

    def slab_for(d):
        return lax.dynamic_slice(stored, (0, ((me_l + d) % n_l) * cells), (slab, cells))

    slabs = [slab_for(0)] + [shift(slab_for(d), "level", d) for d in range(1, n_l)]
    place = jnp.arange(feat, dtype=jnp.int32)
    source = (me_l - place // slab) % n_l
    target = (place % n_vars) * (n_lev * n_l) + source * n_lev + (place % slab) // n_vars
    order = (place[:, None] == target[None, :]).astype(BF)

    def relative(position):
        return (me_l ^ (position // cells)) * cells + position % cells

    moved = jnp.where(neighbours < part, relative(neighbours), neighbours)
    limit = part + 2 * EDGE
    entry = lax.broadcasted_iota(jnp.int32, (limit, 1), 0)
    counts = jnp.zeros((limit, cells), F32)
    for k in range(6):
        counts = counts + (moved[k][None, :] == entry).astype(F32)
    counts = counts.astype(BF)
    valid = jnp.sum((neighbours < limit).astype(F32), axis=0)
    listed = (relative(edge_rows[0].reshape(1, 2 * EDGE)) == entry[:part]).astype(BF)
    placed = mm(enc_in, order).astype(BF)
    slabs, counts, valid, listed, placed, order = lax.optimization_barrier(
        (slabs, counts, valid, listed, placed, order)
    )

    raw, pre_enc, hidden_enc, latent = encode(slabs, placed, enc_out.T)

    table = jnp.concatenate(
        [latent] + [swap(latent, "level", d) for d in range(1, n_l)], axis=1
    )

    columns = mm(order, raw).astype(BF)
    pre_dec = mm_rows(dec_in, latent)
    hidden_dec = jax.nn.silu(pre_dec).astype(BF)
    residual = mm_rows(dec_out, hidden_dec) - columns.astype(F32)
    distortion = jnp.sum(residual * residual, axis=0)
    d_recon = (2.0 * grad_scale * residual).astype(BF)
    term = mm_cells(hidden_dec, d_recon).reshape(n_y, 2, n_l, hidden // (n_h * n_l), feat)
    term = swap_halves(term, 1)
    d_pre_dec = (mm(dec_out, d_recon) * silu_slope(pre_dec)).astype(BF)
    d_latent = mm(dec_in, d_pre_dec)
    half_dec = halves(d_pre_dec, lambda rows: mm_cells(latent, rows))
    table, d_latent, half_dec, term = lax.optimization_barrier((table, d_latent, half_dec, term))

    sent = mm(table, listed).astype(BF)
    halo = jnp.concatenate(
        [shift(sent[:, EDGE:], "horiz", 1), shift(sent[:, :EDGE], "horiz", -1)], axis=1
    )
    total = mm(table, counts[:part])
    halo, total = lax.optimization_barrier((halo, total))
    total = total + mm(halo, counts[part:])
    context_b = (total / valid).astype(BF)
    params = mm_rows(hyper_weight, context_b)
    centre, spread = params[:LATENT], params[LATENT:]
    sigma = scale_offset + jax.nn.softplus(spread)
    scaled = (latent.astype(F32) - centre) / sigma
    rate = jnp.sum(0.5 * scaled * scaled + jnp.log(sigma), axis=0)
    direct = grad_scale * scaled / sigma
    d_spread = grad_scale * (1.0 - scaled * scaled) / sigma * jax.nn.sigmoid(spread)
    d_params = jnp.concatenate([-direct, d_spread], axis=0).astype(BF)
    share = mm(hyper_weight, d_params) / valid
    share = share.astype(BF)

    back = mm_cells(share, counts[part:]).astype(BF)
    to_next, to_prev = back[:, EDGE:], back[:, :EDGE]
    back = jnp.concatenate([shift(to_next, "horiz", 1), shift(to_prev, "horiz", -1)], axis=1)
    own = mm_cells(after(share, to_next, to_prev), counts[:part])
    back, own = lax.optimization_barrier((back, own))
    own = own + mm_cells(back, listed)
    core = lax.axis_index("horiz") % 2
    rows = hidden // n_h
    width = hidden // 2
    half_dec = (half_dec[0] + swap(half_dec[1], "horiz", 1)).astype(BF)
    own, half_dec = lax.optimization_barrier((own, half_dec))
    got = []
    for d in range(1, n_l):
        piece = own[:, d * cells : (d + 1) * cells].astype(BF)
        got.append(swap(jnp.concatenate([piece] + [half_dec] * (d == 1), axis=1), "level", d))
    half_dec = half_dec.astype(F32) + got[0][:, cells:].astype(F32)
    d_neighbour = own[:, :cells]
    for piece in got:
        d_neighbour = d_neighbour + piece[:, :cells].astype(F32)

    term = after(term, own)
    near_dec = pick(term, me_y, 0)
    far = [pick(term, (me_y + d) % n_y, 0).reshape(rows, feat) for d in range(1, n_y)]
    far = to_rows_y([piece.astype(BF) for piece in far])
    context_b, cell_loss = lax.optimization_barrier(
        (context_b, distortion / feat + rate / LATENT, got[0])
    )[:2]
    hyper = mm_cells(context_b, d_params)
    hyper = hyper + swap(hyper, "horiz", 1)
    cell_loss = cell_loss.reshape(-1, EDGE)
    cell_loss = cell_loss + swap(cell_loss, "horiz", 1)
    d_total = (d_latent + direct + d_neighbour).astype(BF)
    d_total, hyper, cell_loss, *far = lax.optimization_barrier((d_total, hyper, cell_loss, *far))

    half_enc = halves(hidden_enc, lambda block: mm_cells(d_total, block))
    half_enc = half_enc[0] + swap(half_enc[1], "horiz", 1)

    def enc_rows(side):
        weight = pick(enc_out.reshape(n_y, 2, rows, LATENT), side, 1).reshape(n_y * rows, LATENT)
        preact = pick(pre_enc.reshape(n_y, 2, rows, cells), side, 1).reshape(n_y * rows, cells)
        d_pre = lax.optimization_barrier((mm(weight, d_total) * silu_slope(preact)).astype(BF))
        return mm_cells(d_pre, columns)

    other = swap(enc_rows(1 - core).astype(BF), "horiz", 1)
    near = (enc_rows(core) + other.astype(F32)).reshape(n_y, rows, feat)
    rider = pack(jnp.concatenate([half_enc, hyper], axis=1), cell_loss)
    sent = [pick(near, (me_y + d) % n_y, 0).astype(BF) for d in range(1, n_y)]
    sent = [jnp.concatenate([piece, rider], axis=0) for piece in sent]
    for piece in far:
        near_dec = near_dec + piece.reshape(near_dec.shape).astype(F32)
    half_dec = half_dec.astype(BF)
    near, near_dec, half_dec, sent = lax.optimization_barrier(
        (pick(near, me_y, 0), near_dec, half_dec, sent)
    )

    arrived = to_rows_y(sent)
    got_dec = []
    for d in range(1, n_l):
        piece = pick(near_dec, me_l ^ d, 0).astype(BF).reshape(LATENT, -1)
        got_dec.append(swap(jnp.concatenate([piece] + [half_dec] * (d == 2), axis=1), "level", d))
    near, arrived, got_dec = lax.optimization_barrier((near, arrived, got_dec))

    for piece in arrived:
        near = near + piece[:rows].astype(F32)
    near = near.reshape(n_l, rows // n_l, feat)
    riders = [rider] + [piece[rows:] for piece in arrived]
    riders = [unpack(piece, LATENT) for piece in riders]
    rider = pack(*(sum_y(list(pieces)) for pieces in zip(*riders)))
    span = got_dec[0].shape[1]
    half_dec = half_dec.astype(F32) + got_dec[1][:, span:].astype(F32)
    few = rows // n_l
    got_enc = []
    for d in range(1, n_l):
        piece = pick(near, me_l ^ d, 0).astype(BF)
        got_enc.append(swap(jnp.concatenate([piece] + [rider] * (d == 1), axis=0), "level", d))
    theirs = got_enc[0][few:]
    bit = 2
    while bit < n_l:
        pieces = [unpack(piece, LATENT) for piece in (rider, theirs)]
        rider = pack(*(tree(list(parts)) for parts in zip(*pieces)))
        theirs = swap(rider, "level", bit)
        bit *= 2
    riders = [rider, theirs]
    half_enc = tree([piece[:LATENT, :width].astype(F32) for piece in riders])
    grad_hyper = tree([piece[:LATENT, width:].astype(F32) for piece in riders])
    cell_loss = tree([piece[LATENT:, : 2 * EDGE].astype(F32) for piece in riders])
    grad_dec_out = pick(near_dec, me_l, 0)
    for piece in got_dec:
        piece = piece[:, :span].reshape(grad_dec_out.shape)
        grad_dec_out = grad_dec_out + piece.astype(F32)
    bit = 4
    while bit < n_l:
        half_dec = half_dec.astype(BF)
        half_dec = half_dec.astype(F32) + swap(half_dec, "level", bit).astype(F32)
        bit *= 2
    half_dec = sum_pairs(half_dec, "horiz", 2, n_h, BF)
    grad_dec_in = both_halves(after(half_dec, *got_enc))
    loss = (jnp.sum(cell_loss) / (part * n_h)).reshape(1)
    grad_enc_out = both_halves(half_enc).T
    grad_enc_in = pick(near, me_l, 0)
    for piece in got_enc:
        grad_enc_in = grad_enc_in + piece[:few].astype(F32)
    return (
        grad_enc_in,
        grad_enc_out,
        grad_dec_in,
        grad_dec_out,
        grad_hyper,
        rate / LATENT,
        loss,
    )


def solution(mesh):
    in_specs = (
        P(None, "level", ("groups", "horiz")),
        P(),
        P(),
        P(),
        P(),
        P(),
        P(None, ("horiz", "level")),
        P("horiz", None, None),
    )
    out_specs = (
        P(("groups", "horiz", "level"), None),
        P("groups", None),
        P("groups", None),
        P(("groups", "horiz", "level"), None),
        P("groups", None),
        P(("groups", "horiz", "level")),
        P("groups"),
    )
    return jax.shard_map(local, mesh=mesh, in_specs=in_specs, out_specs=out_specs, check_vma=False)
```

```python
import functools
import math

import jax
import jax.numpy as jnp
from jax import lax
from jax.experimental import pallas as pl
from jax.experimental.pallas import tpu as pltpu
from jax.sharding import PartitionSpec as P

LATENT = 64
EDGE = 128

BF = jnp.bfloat16
F32 = jnp.float32
scale_offset = 0.1


def mm(left, right):
    return jnp.dot(left, right, preferred_element_type=F32)


def mm_rows(left, right):
    return lax.dot_general(left, right, (((0,), (0,)), ((), ())), preferred_element_type=F32)


def mm_cells(left, right):
    return lax.dot_general(left, right, (((1,), (1,)), ((), ())), preferred_element_type=F32)


def silu_slope(preact):
    squash = jax.nn.sigmoid(preact)
    return squash * (1.0 + preact * (1.0 - squash))


def shift(block, axis, step):
    count = lax.axis_size(axis)
    return lax.ppermute(block, axis, [(i, (i + step) % count) for i in range(count)])


def swap(block, axis, bit):
    count = lax.axis_size(axis)
    return lax.ppermute(block, axis, [(i, i ^ bit) for i in range(count)])


def pick(block, index, dim):
    return lax.dynamic_index_in_dim(block, index, dim, keepdims=False)


def after(value, *others):
    return lax.optimization_barrier((value, *others))[0]


def swap_halves(block, dim):
    core = lax.axis_index("horiz") % 2
    other = swap(pick(block, 1 - core, dim).astype(BF), "horiz", 1)
    return pick(block, core, dim).astype(F32) + other.astype(F32)


def to_rows_y(far):
    return [shift(piece.astype(BF), "horiz", 2 * (d + 1)) for d, piece in enumerate(far)]


def sum_y(pieces):
    count = len(pieces)
    pieces = [piece.astype(F32) for piece in pieces]
    if count > 2:
        me_y = lax.axis_index("horiz") // 2
        stacked = jnp.stack(pieces)
        pieces = [pick(stacked, (me_y - y) % count, 0) for y in range(count)]
    return sum(pieces)


def to_level(block):
    n_l, me_l = lax.axis_size("level"), lax.axis_index("level")
    return [shift(pick(block, (me_l + d) % n_l, 0).astype(BF), "level", d) for d in range(1, n_l)]


def own_level(block, got):
    block = pick(block, lax.axis_index("level"), 0)
    for piece in got:
        block = block + piece.astype(F32)
    return block


def halves(rows, product):
    half = rows.shape[0] // 2
    core = lax.axis_index("horiz") % 2
    mine = lax.dynamic_slice_in_dim(rows, core * half, half, 0)
    theirs = lax.dynamic_slice_in_dim(rows, (1 - core) * half, half, 0)
    return product(mine), product(theirs)


def both_halves(part):
    first = lax.axis_index("horiz") % 2 == 0
    other = swap(part, "horiz", 1)
    return jnp.concatenate([jnp.where(first, part, other), jnp.where(first, other, part)], axis=1)


def pack(block, extra):
    high = lax.reduce_precision(extra, 8, 7)
    both = jnp.concatenate([high, extra - high], axis=1).astype(BF)
    both = jnp.pad(both, ((0, 0), (0, block.shape[1] - both.shape[1])))
    return jnp.concatenate([block.astype(BF), both], axis=0)


def unpack(packed, rows):
    packed = packed.astype(F32)
    return packed[:rows], packed[rows:, :EDGE] + packed[rows:, EDGE : 2 * EDGE]


def sum_pairs(part, axis, first, last, kind):
    bit = first
    while bit < last:
        part = part.astype(kind)
        part = part.astype(F32) + swap(part, axis, bit).astype(F32)
        bit *= 2
    return part


def tree(pieces):
    while len(pieces) > 1:
        pieces = [a + b for a, b in zip(pieces[::2], pieces[1::2])]
    return pieces[0]


def encode_kernel(step, *refs):
    *slab_refs, placed_ref, out_t_ref, raw_ref, pre_ref, hidden_ref, latent_ref = refs
    slab = slab_refs[0].shape[0]
    hidden, cells = pre_ref.shape
    for d, slab_ref in enumerate(slab_refs):
        raw_ref[d * slab : (d + 1) * slab, :] = slab_ref[...]

    latent = jnp.zeros(latent_ref.shape, F32)
    for start in range(0, hidden, step):
        rows = slice(start, start + step)
        preact = jnp.dot(placed_ref[rows, :], raw_ref[...], preferred_element_type=F32)
        pre_ref[rows, :] = preact
        active = (preact * jax.nn.sigmoid(preact)).astype(BF)
        hidden_ref[rows, :] = active
        latent += jnp.dot(out_t_ref[:, rows], active, preferred_element_type=F32)
    latent_ref[...] = latent.astype(BF)


def encode(slabs, placed, out_t):
    slab, cells = slabs[0].shape
    hidden, feat = placed.shape
    vmem = pl.BlockSpec(memory_space=pltpu.VMEM)
    flops = 2 * hidden * cells * (feat + out_t.shape[0])
    size = 4 * hidden * cells + 2 * (hidden * cells + 2 * feat * cells + hidden * feat)
    return pl.pallas_call(
        functools.partial(encode_kernel, hidden // 4),
        out_shape=[
            jax.ShapeDtypeStruct((feat, cells), BF),
            jax.ShapeDtypeStruct((hidden, cells), F32),
            jax.ShapeDtypeStruct((hidden, cells), BF),
            jax.ShapeDtypeStruct((out_t.shape[0], cells), BF),
        ],
        in_specs=[vmem] * (len(slabs) + 2),
        out_specs=[vmem] * 4,
        compiler_params=pltpu.CompilerParams(vmem_limit_bytes=24 * 2**20),
        cost_estimate=pl.CostEstimate(
            flops=flops, bytes_accessed=size, transcendentals=hidden * cells
        ),
    )(*slabs, placed, out_t)


def local(fields, enc_in, enc_out, dec_in, dec_out, hyper_weight, neighbours, edge_rows):
    n_h, n_l = lax.axis_size("horiz"), lax.axis_size("level")
    n_y = n_h // 2
    me_l = lax.axis_index("level")
    me_y = lax.axis_index("horiz") // 2
    n_vars, n_lev, part = fields.shape
    cells = part // n_l
    slab = n_vars * n_lev
    feat = slab * n_l
    hidden = enc_in.shape[0]
    grad_scale = 1.0 / math.sqrt(part * n_h)

    stored = jnp.transpose(fields, (1, 0, 2)).reshape(slab, part)

    def slab_for(d):
        return lax.dynamic_slice(stored, (0, ((me_l + d) % n_l) * cells), (slab, cells))

    slabs = [slab_for(0)] + [shift(slab_for(d), "level", d) for d in range(1, n_l)]
    place = jnp.arange(feat, dtype=jnp.int32)
    source = (me_l - place // slab) % n_l
    target = (place % n_vars) * (n_lev * n_l) + source * n_lev + (place % slab) // n_vars
    order = (place[:, None] == target[None, :]).astype(BF)

    def relative(position):
        return (me_l ^ (position // cells)) * cells + position % cells

    moved = jnp.where(neighbours < part, relative(neighbours), neighbours)
    limit = part + 2 * EDGE
    entry = lax.broadcasted_iota(jnp.int32, (limit, 1), 0)
    counts = jnp.zeros((limit, cells), F32)
    for k in range(6):
        counts = counts + (moved[k][None, :] == entry).astype(F32)
    counts = counts.astype(BF)
    valid = jnp.sum((neighbours < limit).astype(F32), axis=0)
    listed = (relative(edge_rows[0].reshape(1, 2 * EDGE)) == entry[:part]).astype(BF)
    placed = mm(enc_in, order).astype(BF)
    slabs, counts, valid, listed, placed, order = lax.optimization_barrier(
        (slabs, counts, valid, listed, placed, order)
    )

    raw, pre_enc, hidden_enc, latent = encode(slabs, placed, enc_out.T)

    table = jnp.concatenate(
        [latent] + [swap(latent, "level", d) for d in range(1, n_l)], axis=1
    )

    columns = mm(order, raw).astype(BF)
    pre_dec = mm_rows(dec_in, latent)
    hidden_dec = jax.nn.silu(pre_dec).astype(BF)
    residual = mm_rows(dec_out, hidden_dec) - columns.astype(F32)
    distortion = jnp.sum(residual * residual, axis=0)
    d_recon = (2.0 * grad_scale * residual).astype(BF)
    term = mm_cells(hidden_dec, d_recon).reshape(n_y, 2, n_l, hidden // (n_h * n_l), feat)
    term = swap_halves(term, 1)
    d_pre_dec = (mm(dec_out, d_recon) * silu_slope(pre_dec)).astype(BF)
    d_latent = mm(dec_in, d_pre_dec)
    half_dec = halves(d_pre_dec, lambda rows: mm_cells(latent, rows))
    table, d_latent, half_dec, term = lax.optimization_barrier((table, d_latent, half_dec, term))

    sent = mm(table, listed).astype(BF)
    halo = jnp.concatenate(
        [shift(sent[:, EDGE:], "horiz", 1), shift(sent[:, :EDGE], "horiz", -1)], axis=1
    )
    total = mm(table, counts[:part])
    halo, total = lax.optimization_barrier((halo, total))
    total = total + mm(halo, counts[part:])
    context_b = (total / valid).astype(BF)
    params = mm_rows(hyper_weight, context_b)
    centre, spread = params[:LATENT], params[LATENT:]
    sigma = scale_offset + jax.nn.softplus(spread)
    scaled = (latent.astype(F32) - centre) / sigma
    rate = jnp.sum(0.5 * scaled * scaled + jnp.log(sigma), axis=0)
    direct = grad_scale * scaled / sigma
    d_spread = grad_scale * (1.0 - scaled * scaled) / sigma * jax.nn.sigmoid(spread)
    d_params = jnp.concatenate([-direct, d_spread], axis=0).astype(BF)
    share = mm(hyper_weight, d_params) / valid
    share = share.astype(BF)

    back = mm_cells(share, counts[part:]).astype(BF)
    to_next, to_prev = back[:, EDGE:], back[:, :EDGE]
    back = jnp.concatenate([shift(to_next, "horiz", 1), shift(to_prev, "horiz", -1)], axis=1)
    own = mm_cells(after(share, to_next, to_prev), counts[:part])
    back, own = lax.optimization_barrier((back, own))
    own = own + mm_cells(back, listed)
    core = lax.axis_index("horiz") % 2
    rows = hidden // n_h
    width = hidden // 2
    half_dec = (half_dec[0] + swap(half_dec[1], "horiz", 1)).astype(BF)
    own, half_dec = lax.optimization_barrier((own, half_dec))
    got = []
    for d in range(1, n_l):
        piece = own[:, d * cells : (d + 1) * cells].astype(BF)
        got.append(swap(jnp.concatenate([piece] + [half_dec] * (d == 1), axis=1), "level", d))
    half_dec = half_dec.astype(F32) + got[0][:, cells:].astype(F32)
    d_neighbour = own[:, :cells]
    for piece in got:
        d_neighbour = d_neighbour + piece[:, :cells].astype(F32)

    term = after(term, own)
    near_dec = pick(term, me_y, 0)
    far = [pick(term, (me_y + d) % n_y, 0).reshape(rows, feat) for d in range(1, n_y)]
    far = to_rows_y([piece.astype(BF) for piece in far])
    context_b, cell_loss, pre_enc = lax.optimization_barrier(
        (context_b, distortion / feat + rate / LATENT, pre_enc, got[0])
    )[:3]
    slope = silu_slope(pre_enc)
    hyper = mm_cells(context_b, d_params)
    hyper = hyper + swap(hyper, "horiz", 1)
    cell_loss = cell_loss.reshape(-1, EDGE)
    cell_loss = cell_loss + swap(cell_loss, "horiz", 1)
    d_total = (d_latent + direct + d_neighbour).astype(BF)
    d_total, slope, hyper, cell_loss, *far = lax.optimization_barrier(
        (d_total, slope, hyper, cell_loss, *far)
    )

    half_enc = halves(hidden_enc, lambda block: mm_cells(d_total, block))
    half_enc = half_enc[0] + swap(half_enc[1], "horiz", 1)

    def enc_rows(side):
        weight = pick(enc_out.reshape(n_y, 2, rows, LATENT), side, 1).reshape(n_y * rows, LATENT)
        factor = pick(slope.reshape(n_y, 2, rows, cells), side, 1).reshape(n_y * rows, cells)
        d_pre = lax.optimization_barrier((mm(weight, d_total) * factor).astype(BF))
        return mm_cells(d_pre, columns)

    other = swap(enc_rows(1 - core).astype(BF), "horiz", 1)
    near = (enc_rows(core) + other.astype(F32)).reshape(n_y, rows, feat)
    rider = pack(jnp.concatenate([half_enc, hyper], axis=1), cell_loss)
    sent = [pick(near, (me_y + d) % n_y, 0).astype(BF) for d in range(1, n_y)]
    sent = [jnp.concatenate([piece, rider], axis=0) for piece in sent]
    for piece in far:
        near_dec = near_dec + piece.reshape(near_dec.shape).astype(F32)
    half_dec = half_dec.astype(BF)
    near, near_dec, half_dec, sent = lax.optimization_barrier(
        (pick(near, me_y, 0), near_dec, half_dec, sent)
    )

    arrived = to_rows_y(sent)
    got_dec = []
    for d in range(1, n_l):
        piece = pick(near_dec, me_l ^ d, 0).astype(BF).reshape(LATENT, -1)
        got_dec.append(swap(jnp.concatenate([piece] + [half_dec] * (d == 2), axis=1), "level", d))
    near, arrived, got_dec = lax.optimization_barrier((near, arrived, got_dec))

    for piece in arrived:
        near = near + piece[:rows].astype(F32)
    near = near.reshape(n_l, rows // n_l, feat)
    riders = [rider] + [piece[rows:] for piece in arrived]
    riders = [unpack(piece, LATENT) for piece in riders]
    rider = pack(*(sum_y(list(pieces)) for pieces in zip(*riders)))
    span = got_dec[0].shape[1]
    half_dec = half_dec.astype(F32) + got_dec[1][:, span:].astype(F32)
    few = rows // n_l
    got_enc = []
    for d in range(1, n_l):
        piece = pick(near, me_l ^ d, 0).astype(BF)
        got_enc.append(swap(jnp.concatenate([piece] + [rider] * (d == 1), axis=0), "level", d))
    theirs = got_enc[0][few:]
    bit = 2
    while bit < n_l:
        pieces = [unpack(piece, LATENT) for piece in (rider, theirs)]
        rider = pack(*(tree(list(parts)) for parts in zip(*pieces)))
        theirs = swap(rider, "level", bit)
        bit *= 2
    riders = [rider, theirs]
    half_enc = tree([piece[:LATENT, :width].astype(F32) for piece in riders])
    grad_hyper = tree([piece[:LATENT, width:].astype(F32) for piece in riders])
    cell_loss = tree([piece[LATENT:, : 2 * EDGE].astype(F32) for piece in riders])
    grad_dec_out = pick(near_dec, me_l, 0)
    for piece in got_dec:
        piece = piece[:, :span].reshape(grad_dec_out.shape)
        grad_dec_out = grad_dec_out + piece.astype(F32)
    bit = 4
    while bit < n_l:
        half_dec = half_dec.astype(BF)
        half_dec = half_dec.astype(F32) + swap(half_dec, "level", bit).astype(F32)
        bit *= 2
    half_dec = sum_pairs(half_dec, "horiz", 2, n_h, BF)
    grad_dec_in = both_halves(after(half_dec, *got_enc))
    loss = (jnp.sum(cell_loss) / (part * n_h)).reshape(1)
    grad_enc_out = both_halves(half_enc).T
    grad_enc_in = pick(near, me_l, 0)
    for piece in got_enc:
        grad_enc_in = grad_enc_in + piece[:few].astype(F32)
    return (
        grad_enc_in,
        grad_enc_out,
        grad_dec_in,
        grad_dec_out,
        grad_hyper,
        rate / LATENT,
        loss,
    )


def solution(mesh):
    in_specs = (
        P(None, "level", ("groups", "horiz")),
        P(),
        P(),
        P(),
        P(),
        P(),
        P(None, ("horiz", "level")),
        P("horiz", None, None),
    )
    out_specs = (
        P(("groups", "horiz", "level"), None),
        P("groups", None),
        P("groups", None),
        P(("groups", "horiz", "level"), None),
        P("groups", None),
        P(("groups", "horiz", "level")),
        P("groups"),
    )
    return jax.shard_map(local, mesh=mesh, in_specs=in_specs, out_specs=out_specs, check_vma=False)
```

```python
import functools
import math

import jax
import jax.numpy as jnp
from jax import lax
from jax.experimental import pallas as pl
from jax.experimental.pallas import tpu as pltpu
from jax.sharding import PartitionSpec as P

LATENT = 64
EDGE = 128

BF = jnp.bfloat16
F32 = jnp.float32
scale_offset = 0.1


def mm(left, right):
    return jnp.dot(left, right, preferred_element_type=F32)


def mm_rows(left, right):
    return lax.dot_general(left, right, (((0,), (0,)), ((), ())), preferred_element_type=F32)


def mm_cells(left, right):
    return lax.dot_general(left, right, (((1,), (1,)), ((), ())), preferred_element_type=F32)


def silu_slope(preact):
    squash = jax.nn.sigmoid(preact)
    return squash * (1.0 + preact * (1.0 - squash))


def shift(block, axis, step):
    count = lax.axis_size(axis)
    return lax.ppermute(block, axis, [(i, (i + step) % count) for i in range(count)])


def swap(block, axis, bit):
    count = lax.axis_size(axis)
    return lax.ppermute(block, axis, [(i, i ^ bit) for i in range(count)])


def pick(block, index, dim):
    return lax.dynamic_index_in_dim(block, index, dim, keepdims=False)


def after(value, *others):
    return lax.optimization_barrier((value, *others))[0]


def swap_halves(block, dim):
    core = lax.axis_index("horiz") % 2
    other = swap(pick(block, 1 - core, dim).astype(BF), "horiz", 1)
    return pick(block, core, dim).astype(F32) + other.astype(F32)


def to_rows_y(far):
    return [shift(piece.astype(BF), "horiz", 2 * (d + 1)) for d, piece in enumerate(far)]


def sum_y(pieces):
    count = len(pieces)
    pieces = [piece.astype(F32) for piece in pieces]
    if count > 2:
        me_y = lax.axis_index("horiz") // 2
        stacked = jnp.stack(pieces)
        pieces = [pick(stacked, (me_y - y) % count, 0) for y in range(count)]
    return sum(pieces)


def to_level(block):
    n_l, me_l = lax.axis_size("level"), lax.axis_index("level")
    return [shift(pick(block, (me_l + d) % n_l, 0).astype(BF), "level", d) for d in range(1, n_l)]


def own_level(block, got):
    block = pick(block, lax.axis_index("level"), 0)
    for piece in got:
        block = block + piece.astype(F32)
    return block


def halves(rows, product):
    half = rows.shape[0] // 2
    core = lax.axis_index("horiz") % 2
    mine = lax.dynamic_slice_in_dim(rows, core * half, half, 0)
    theirs = lax.dynamic_slice_in_dim(rows, (1 - core) * half, half, 0)
    return product(mine), product(theirs)


def both_halves(part):
    first = lax.axis_index("horiz") % 2 == 0
    other = swap(part, "horiz", 1)
    return jnp.concatenate([jnp.where(first, part, other), jnp.where(first, other, part)], axis=1)


def pack(block, extra):
    high = lax.reduce_precision(extra, 8, 7)
    both = jnp.concatenate([high, extra - high], axis=1).astype(BF)
    both = jnp.pad(both, ((0, 0), (0, block.shape[1] - both.shape[1])))
    return jnp.concatenate([block.astype(BF), both], axis=0)


def unpack(packed, rows):
    packed = packed.astype(F32)
    return packed[:rows], packed[rows:, :EDGE] + packed[rows:, EDGE : 2 * EDGE]


def sum_pairs(part, axis, first, last, kind):
    bit = first
    while bit < last:
        part = part.astype(kind)
        part = part.astype(F32) + swap(part, axis, bit).astype(F32)
        bit *= 2
    return part


def tree(pieces):
    while len(pieces) > 1:
        pieces = [a + b for a, b in zip(pieces[::2], pieces[1::2])]
    return pieces[0]


def encode_kernel(step, *refs):
    *slab_refs, placed_ref, out_t_ref, raw_ref, pre_ref, hidden_ref, latent_ref = refs
    slab = slab_refs[0].shape[0]
    hidden, cells = pre_ref.shape
    for d, slab_ref in enumerate(slab_refs):
        raw_ref[d * slab : (d + 1) * slab, :] = slab_ref[...]

    latent = jnp.zeros(latent_ref.shape, F32)
    for start in range(0, hidden, step):
        rows = slice(start, start + step)
        preact = jnp.dot(placed_ref[rows, :], raw_ref[...], preferred_element_type=F32)
        pre_ref[rows, :] = preact
        active = (preact * jax.nn.sigmoid(preact)).astype(BF)
        hidden_ref[rows, :] = active
        latent += jnp.dot(out_t_ref[:, rows], active, preferred_element_type=F32)
    latent_ref[...] = latent.astype(BF)


def encode(slabs, placed, out_t):
    slab, cells = slabs[0].shape
    hidden, feat = placed.shape
    vmem = pl.BlockSpec(memory_space=pltpu.VMEM)
    flops = 2 * hidden * cells * (feat + out_t.shape[0])
    size = 4 * hidden * cells + 2 * (hidden * cells + 2 * feat * cells + hidden * feat)
    return pl.pallas_call(
        functools.partial(encode_kernel, hidden // 4),
        out_shape=[
            jax.ShapeDtypeStruct((feat, cells), BF),
            jax.ShapeDtypeStruct((hidden, cells), F32),
            jax.ShapeDtypeStruct((hidden, cells), BF),
            jax.ShapeDtypeStruct((out_t.shape[0], cells), BF),
        ],
        in_specs=[vmem] * (len(slabs) + 2),
        out_specs=[vmem] * 4,
        compiler_params=pltpu.CompilerParams(vmem_limit_bytes=24 * 2**20),
        cost_estimate=pl.CostEstimate(
            flops=flops, bytes_accessed=size, transcendentals=hidden * cells
        ),
    )(*slabs, placed, out_t)


def local(fields, enc_in, enc_out, dec_in, dec_out, hyper_weight, neighbours, edge_rows):
    n_h, n_l = lax.axis_size("horiz"), lax.axis_size("level")
    n_y = n_h // 2
    me_l = lax.axis_index("level")
    me_y = lax.axis_index("horiz") // 2
    n_vars, n_lev, part = fields.shape
    cells = part // n_l
    slab = n_vars * n_lev
    feat = slab * n_l
    hidden = enc_in.shape[0]
    grad_scale = 1.0 / math.sqrt(part * n_h)

    stored = jnp.transpose(fields, (1, 0, 2)).reshape(slab, part)

    def slab_for(d):
        return lax.dynamic_slice(stored, (0, ((me_l + d) % n_l) * cells), (slab, cells))

    slabs = [slab_for(0)] + [shift(slab_for(d), "level", d) for d in range(1, n_l)]
    place = jnp.arange(feat, dtype=jnp.int32)
    source = (me_l - place // slab) % n_l
    target = (place % n_vars) * (n_lev * n_l) + source * n_lev + (place % slab) // n_vars
    order = (place[:, None] == target[None, :]).astype(BF)

    def relative(position):
        return (me_l ^ (position // cells)) * cells + position % cells

    moved = jnp.where(neighbours < part, relative(neighbours), neighbours)
    limit = part + 2 * EDGE
    entry = lax.broadcasted_iota(jnp.int32, (limit, 1), 0)
    counts = jnp.zeros((limit, cells), F32)
    for k in range(6):
        counts = counts + (moved[k][None, :] == entry).astype(F32)
    counts = counts.astype(BF)
    valid = jnp.sum((neighbours < limit).astype(F32), axis=0)
    listed = (relative(edge_rows[0].reshape(1, 2 * EDGE)) == entry[:part]).astype(BF)
    placed = mm(enc_in, order).astype(BF)
    slabs, counts, valid, listed, placed, order = lax.optimization_barrier(
        (slabs, counts, valid, listed, placed, order)
    )

    raw, pre_enc, hidden_enc, latent = encode(slabs, placed, enc_out.T)

    table = jnp.concatenate(
        [latent] + [swap(latent, "level", d) for d in range(1, n_l)], axis=1
    )

    columns = mm(order, raw).astype(BF)
    pre_dec = mm_rows(dec_in, latent)
    hidden_dec = jax.nn.silu(pre_dec).astype(BF)
    residual = mm_rows(dec_out, hidden_dec) - columns.astype(F32)
    distortion = jnp.sum(residual * residual, axis=0)
    d_recon = (2.0 * grad_scale * residual).astype(BF)
    term = mm_cells(hidden_dec, d_recon).reshape(n_y, 2, n_l, hidden // (n_h * n_l), feat)
    term = swap_halves(term, 1)
    d_pre_dec = (mm(dec_out, d_recon) * silu_slope(pre_dec)).astype(BF)
    d_latent = mm(dec_in, d_pre_dec)
    half_dec = halves(d_pre_dec, lambda rows: mm_cells(latent, rows))
    table, d_latent, half_dec, term = lax.optimization_barrier((table, d_latent, half_dec, term))

    sent = mm(table, listed).astype(BF)
    halo = jnp.concatenate(
        [shift(sent[:, EDGE:], "horiz", 1), shift(sent[:, :EDGE], "horiz", -1)], axis=1
    )
    total = mm(table, counts[:part])
    halo, total = lax.optimization_barrier((halo, total))
    total = total + mm(halo, counts[part:])
    context_b = (total / valid).astype(BF)
    params = mm_rows(hyper_weight, context_b)
    centre, spread = params[:LATENT], params[LATENT:]
    sigma = scale_offset + jax.nn.softplus(spread)
    scaled = (latent.astype(F32) - centre) / sigma
    rate = jnp.sum(0.5 * scaled * scaled + jnp.log(sigma), axis=0)
    direct = grad_scale * scaled / sigma
    d_spread = grad_scale * (1.0 - scaled * scaled) / sigma * jax.nn.sigmoid(spread)
    d_params = jnp.concatenate([-direct, d_spread], axis=0).astype(BF)
    share = mm(hyper_weight, d_params) / valid
    share = share.astype(BF)

    back = mm_cells(share, counts[part:]).astype(BF)
    to_next, to_prev = back[:, EDGE:], back[:, :EDGE]
    back = jnp.concatenate([shift(to_next, "horiz", 1), shift(to_prev, "horiz", -1)], axis=1)
    own = mm_cells(after(share, to_next, to_prev), counts[:part])
    back, own = lax.optimization_barrier((back, own))
    own = own + mm_cells(back, listed)
    core = lax.axis_index("horiz") % 2
    rows = hidden // n_h
    width = hidden // 2
    half_dec = (half_dec[0] + swap(half_dec[1], "horiz", 1)).astype(BF)
    own, half_dec = lax.optimization_barrier((own, half_dec))
    got = []
    for d in range(1, n_l):
        piece = own[:, d * cells : (d + 1) * cells].astype(BF)
        got.append(swap(jnp.concatenate([piece] + [half_dec] * (d == 1), axis=1), "level", d))
    half_dec = half_dec.astype(F32) + got[0][:, cells:].astype(F32)
    d_neighbour = own[:, :cells]
    for piece in got:
        d_neighbour = d_neighbour + piece[:, :cells].astype(F32)

    term = after(term, own)
    near_dec = pick(term, me_y, 0)
    far = [pick(term, (me_y + d) % n_y, 0).reshape(rows, feat) for d in range(1, n_y)]
    far = to_rows_y([piece.astype(BF) for piece in far])
    context_b, cell_loss, pre_enc = lax.optimization_barrier(
        (context_b, distortion / feat + rate / LATENT, pre_enc, got[0])
    )[:3]
    slope = silu_slope(pre_enc).reshape(n_y, 2, rows, cells)
    weight = enc_out.reshape(n_y, 2, rows, LATENT)
    weight = [pick(weight, side, 1).reshape(n_y * rows, LATENT) for side in (core, 1 - core)]
    slope = [pick(slope, side, 1).reshape(n_y * rows, cells) for side in (core, 1 - core)]
    hyper = mm_cells(context_b, d_params)
    hyper = hyper + swap(hyper, "horiz", 1)
    cell_loss = cell_loss.reshape(-1, EDGE)
    cell_loss = cell_loss + swap(cell_loss, "horiz", 1)
    d_total = (d_latent + direct + d_neighbour).astype(BF)
    d_total, slope, weight, hyper, cell_loss, *far = lax.optimization_barrier(
        (d_total, slope, weight, hyper, cell_loss, *far)
    )

    half_enc = halves(hidden_enc, lambda block: mm_cells(d_total, block))
    half_enc = half_enc[0] + swap(half_enc[1], "horiz", 1)

    def enc_rows(side):
        d_pre = (mm(weight[side], d_total) * slope[side]).astype(BF)
        return mm_cells(lax.optimization_barrier(d_pre), columns)

    other = swap(enc_rows(1).astype(BF), "horiz", 1)
    near = (enc_rows(0) + other.astype(F32)).reshape(n_y, rows, feat)
    rider = pack(jnp.concatenate([half_enc, hyper], axis=1), cell_loss)
    sent = [pick(near, (me_y + d) % n_y, 0).astype(BF) for d in range(1, n_y)]
    sent = [jnp.concatenate([piece, rider], axis=0) for piece in sent]
    for piece in far:
        near_dec = near_dec + piece.reshape(near_dec.shape).astype(F32)
    half_dec = half_dec.astype(BF)
    near, near_dec, half_dec, sent = lax.optimization_barrier(
        (pick(near, me_y, 0), near_dec, half_dec, sent)
    )

    arrived = to_rows_y(sent)
    got_dec = []
    for d in range(1, n_l):
        piece = pick(near_dec, me_l ^ d, 0).astype(BF).reshape(LATENT, -1)
        got_dec.append(swap(jnp.concatenate([piece] + [half_dec] * (d == 2), axis=1), "level", d))
    near, arrived, got_dec = lax.optimization_barrier((near, arrived, got_dec))

    for piece in arrived:
        near = near + piece[:rows].astype(F32)
    near = near.reshape(n_l, rows // n_l, feat)
    riders = [rider] + [piece[rows:] for piece in arrived]
    riders = [unpack(piece, LATENT) for piece in riders]
    rider = pack(*(sum_y(list(pieces)) for pieces in zip(*riders)))
    span = got_dec[0].shape[1]
    half_dec = half_dec.astype(F32) + got_dec[1][:, span:].astype(F32)
    few = rows // n_l
    got_enc = []
    for d in range(1, n_l):
        piece = pick(near, me_l ^ d, 0).astype(BF)
        got_enc.append(swap(jnp.concatenate([piece] + [rider] * (d == 1), axis=0), "level", d))
    theirs = got_enc[0][few:]
    bit = 2
    while bit < n_l:
        pieces = [unpack(piece, LATENT) for piece in (rider, theirs)]
        rider = pack(*(tree(list(parts)) for parts in zip(*pieces)))
        theirs = swap(rider, "level", bit)
        bit *= 2
    riders = [rider, theirs]
    half_enc = tree([piece[:LATENT, :width].astype(F32) for piece in riders])
    grad_hyper = tree([piece[:LATENT, width:].astype(F32) for piece in riders])
    cell_loss = tree([piece[LATENT:, : 2 * EDGE].astype(F32) for piece in riders])
    grad_dec_out = pick(near_dec, me_l, 0)
    for piece in got_dec:
        piece = piece[:, :span].reshape(grad_dec_out.shape)
        grad_dec_out = grad_dec_out + piece.astype(F32)
    bit = 4
    while bit < n_l:
        half_dec = half_dec.astype(BF)
        half_dec = half_dec.astype(F32) + swap(half_dec, "level", bit).astype(F32)
        bit *= 2
    half_dec = sum_pairs(half_dec, "horiz", 2, n_h, BF)
    grad_dec_in = both_halves(after(half_dec, got_enc[0]))
    loss = (jnp.sum(cell_loss) / (part * n_h)).reshape(1)
    grad_enc_out = both_halves(half_enc).T
    grad_enc_in = pick(near, me_l, 0)
    for piece in got_enc:
        grad_enc_in = grad_enc_in + piece[:few].astype(F32)
    return (
        grad_enc_in,
        grad_enc_out,
        grad_dec_in,
        grad_dec_out,
        grad_hyper,
        rate / LATENT,
        loss,
    )


def solution(mesh):
    in_specs = (
        P(None, "level", ("groups", "horiz")),
        P(),
        P(),
        P(),
        P(),
        P(),
        P(None, ("horiz", "level")),
        P("horiz", None, None),
    )
    out_specs = (
        P(("groups", "horiz", "level"), None),
        P("groups", None),
        P("groups", None),
        P(("groups", "horiz", "level"), None),
        P("groups", None),
        P(("groups", "horiz", "level")),
        P("groups"),
    )
    return jax.shard_map(local, mesh=mesh, in_specs=in_specs, out_specs=out_specs, check_vma=False)
```
